32 devices in a mesh: seq: 4 (over z), batch: 8 (over y, x, core).
Axes of the slice: x: 2, y: 2, z: 4, core: 2. Of those that a mesh axis runs over, the one named last changes fastest.
Arguments:
- tokens: bfloat16 [64, 1024, 512], P('batch', 'seq'), may hold values from -6 to 6
- cotangent: bfloat16 [64, 1024, 512], P('batch', 'seq'), may hold values from -6 to 6
- expert_index: int32 [64, 1024, 2], P('batch', 'seq'), may hold values from 0 to 7, all different within a row
- segments: int32 [64, 1024], P('batch'), may hold values from 0 to 32, as said below
- ln1_gain: bfloat16 [512], P(('seq', 'batch')), may hold values from 0.5 to 1.5
- ln1_bias: bfloat16 [512], P(('seq', 'batch')), may hold values from -4 to 4
- w_router: bfloat16 [512, 8], P(('seq', 'batch')), may hold values from -0.1875 to 0.1875
- w_query: bfloat16 [512, 512], P(('seq', 'batch')), may hold values from -0.25 to 0.25
- b_query: bfloat16 [512], P(('seq', 'batch')), may hold values from -4 to 4
- w_keyval: bfloat16 [512, 128], P(('seq', 'batch')), may hold values from -0.25 to 0.25
- w_out: bfloat16 [512, 512], P(('seq', 'batch')), may hold values from -2 to 2
- b_out: bfloat16 [512], P(('seq', 'batch')), may hold values from -4 to 4
- ln2_gain: bfloat16 [512], P(('seq', 'batch')), may hold values from 0.5 to 1.5
- ln2_bias: bfloat16 [512], P(('seq', 'batch')), may hold values from -4 to 4
- w_up: bfloat16 [512, 2048], P(('seq', 'batch')), may hold values from -0.25 to 0.25
- b_up: bfloat16 [2048], P(('seq', 'batch')), may hold values from -4 to 4
- w_down: bfloat16 [2048, 512], P(('seq', 'batch')), may hold values from -0.125 to 0.125
- b_down: bfloat16 [512], P(('seq', 'batch')), may hold values from -4 to 4
Outputs:
- output: bfloat16 [64, 1024, 512], P('batch', 'seq')
- grad_tokens: bfloat16 [64, 1024, 512], P('batch', 'seq')
- grad_ln1_gain: float32 [512], P(('seq', 'batch'))
- grad_ln1_bias: float32 [512], P(('seq', 'batch'))
- grad_w_router: float32 [512, 8], P(('seq', 'batch'))
- grad_w_query: float32 [512, 512], P(('seq', 'batch'))
- grad_b_query: float32 [512], P(('seq', 'batch'))
- grad_w_keyval: float32 [512, 128], P(('seq', 'batch'))
- grad_w_out: float32 [512, 512], P(('seq', 'batch'))
- grad_b_out: float32 [512], P(('seq', 'batch'))
- grad_ln2_gain: float32 [512], P(('seq', 'batch'))
- grad_ln2_bias: float32 [512], P(('seq', 'batch'))
- grad_w_up: float32 [512, 2048], P(('seq', 'batch'))
- grad_b_up: float32 [2048], P(('seq', 'batch'))
- grad_w_down: float32 [2048, 512], P(('seq', 'batch'))
- grad_b_down: float32 [512], P(('seq', 'batch'))
The draws below stay inside these ranges and needn't reach their ends.
Inputs may be any that keep to these rules, and one draw needn't show every extreme that they name: `segments`: each row's segment numbers start at 0, rise by 0 or 1 from one position to the next and end at 32; in one row of each aligned group of 8 rows one segment covers positions 128 to 895.
All inputs are finite; a program needn't handle non-finite values.
Results may differ from the reference program's by a relative error of at most 0.012.
Values may be sent and summed in bfloat16 or wider, within the bound.
No kernel may reach another device: no remote copies, remote signals or barrier semaphores. Data moves between devices by JAX's collectives and lax.ppermute only.
A program may use at most 128 MiB of HBM per device.

```python
import jax
import jax.numpy as jnp
from jax import lax

D = 512
FF = 2048
HD = 64
EXPERTS = 8
TOPK = 2
SEQ_LEN = 1024
ROWS_DEV = 8
ROWS = 64


def draw_segments(key, part):
    key = jax.random.fold_in(key, 11)
    key_rate, key_roll, key_pick = jax.random.split(key, 3)
    groups = ROWS // ROWS_DEV
    cut_rate = jax.random.randint(key_rate, (ROWS, 1), 8, 64)
    rolls = jax.random.randint(key_roll, (ROWS, SEQ_LEN), 0, 1 << 20)
    cuts = rolls % cut_rate == 0
    position = jnp.arange(SEQ_LEN, dtype=jnp.int32)[None, :]
    picked = jax.random.randint(key_pick, (groups, 1), 0, ROWS_DEV)
    in_group = jnp.arange(ROWS, dtype=jnp.int32).reshape(groups, ROWS_DEV) % ROWS_DEV
    long_row = (in_group == picked).reshape(ROWS, 1)
    band = (position >= SEQ_LEN // 8) & (position < SEQ_LEN - SEQ_LEN // 8)
    tail = (position >= SEQ_LEN - SEQ_LEN // 8) & (position % 4 == 0)
    cuts = cuts & jnp.logical_not(long_row & band) & (position > 0) | tail
    counted = jnp.cumsum(cuts.astype(jnp.int32), axis=1).astype(jnp.int32)
    return jnp.minimum(counted, SEQ_LEN // 32).astype(jnp.int32)


def level_of(stream_key, shape, cuts, least, high):
    level, own = 1.0, jax.random.fold_in(stream_key, 6)
    for dim, parts in cuts:
        draws = jnp.exp(jax.random.uniform(jax.random.fold_in(own, dim), (parts,), jnp.float32, least / len(cuts), high / len(cuts)))
        level = level * jnp.repeat(draws, shape[dim] // parts).reshape([-1 if axis == dim else 1 for axis in range(len(shape))])
    return level


def different_ones(stream_key, rows, count, top, lift):
    sequence = jax.random.permutation(jax.random.fold_in(stream_key, 1), count)
    boost = sequence
    for power in range(3):
        boost = boost * boost // count
    boost = boost * lift // count
    tickets = jax.random.randint(jax.random.fold_in(stream_key, 2), (rows, count), 0, 4096) + boost
    holders = jax.random.permutation(jax.random.fold_in(stream_key, 3), rows)[jnp.arange(count) % rows]
    tickets = jnp.where(jnp.arange(rows)[:, None] == holders[None, :], 1 << 14, tickets)
    priority = tickets * count + jnp.arange(count)
    return lax.top_k(priority.astype(jnp.int32), top)[1].astype(jnp.int32)


def bell_draw(stream_key, dims, width, most, cuts=(), kind=jnp.bfloat16):
    level = level_of(stream_key, dims, cuts, -0.22, 0.18) if cuts else 1.0
    values = jax.random.normal(stream_key, dims, jnp.float32) * width * level
    return jnp.minimum(jnp.maximum(values, -most), most).astype(kind)


def setup_inputs(seed: int = 0) -> dict:
    keys = jax.random.split(jax.random.key(seed), 19)
    tokens = bell_draw(keys[0], (ROWS, SEQ_LEN, D), 1.0, 6.0, ((0, 8), (1, 4)))
    cotangent = bell_draw(keys[1], (ROWS, SEQ_LEN, D), 1.0, 6.0, ((0, 8), (1, 4)))
    expert_index = different_ones(keys[2], ROWS * SEQ_LEN, EXPERTS, TOPK, 2048).reshape((ROWS, SEQ_LEN, TOPK))
    segments = draw_segments(jax.random.fold_in(keys[18], 71), 0)
    ln1_gain = jnp.clip(1.0 + 0.1 * jax.random.normal(keys[4], (D,), jnp.float32), 0.5, 1.5).astype(jnp.bfloat16)
    ln1_bias = bell_draw(keys[5], (D,), 0.3, 4.0, ((0, 32),))
    w_router = bell_draw(keys[6], (D, EXPERTS), (2 * D) ** -0.5, 0.1875, ((0, 32),))
    w_query = bell_draw(keys[7], (D, EXPERTS * HD), D ** -0.5, 0.25, ((0, 32),))
    b_query = bell_draw(keys[8], (EXPERTS * HD,), 0.3, 4.0, ((0, 32),))
    w_keyval = bell_draw(keys[9], (D, 2 * HD), D ** -0.5, 0.25, ((0, 32),))
    w_out = bell_draw(keys[10], (EXPERTS * HD, D), (HD // 8) ** -0.5, 2.0, ((0, 32),))
    b_out = bell_draw(keys[11], (D,), 0.3, 4.0, ((0, 32),))
    ln2_gain = jnp.clip(1.0 + 0.1 * jax.random.normal(keys[12], (D,), jnp.float32), 0.5, 1.5).astype(jnp.bfloat16)
    ln2_bias = bell_draw(keys[13], (D,), 0.3, 4.0, ((0, 32),))
    w_up = bell_draw(keys[14], (D, FF), D ** -0.5, 0.25, ((0, 32),))
    b_up = bell_draw(keys[15], (FF,), 0.3, 4.0, ((0, 32),))
    w_down = bell_draw(keys[16], (FF, D), FF ** -0.5, 0.125, ((0, 32),))
    b_down = bell_draw(keys[17], (D,), 0.3, 4.0, ((0, 32),))
    return dict(tokens=tokens, cotangent=cotangent, expert_index=expert_index, segments=segments, ln1_gain=ln1_gain, ln1_bias=ln1_bias, w_router=w_router, w_query=w_query, b_query=b_query, w_keyval=w_keyval, w_out=w_out, b_out=b_out, ln2_gain=ln2_gain, ln2_bias=ln2_bias, w_up=w_up, b_up=b_up, w_down=w_down, b_down=b_down)


@jax.custom_vjp
def low(v):
    return lax.optimization_barrier(v.astype(jnp.bfloat16)).astype(jnp.float32)

@jax.custom_vjp
def low_back(v):
    return v

def low_keep(v):
    return (low(v), None)

def low_pass(kept, grad):
    return (grad,)

def back_keep(v):
    return (v, None)

def back_low(kept, grad):
    return (low(grad),)
low.defvjp(low_keep, low_pass)
low_back.defvjp(back_keep, back_low)
HIGHEST = lax.Precision.HIGHEST
epsilon = 1e-05
neg_large = -1e+30

def normalize(values, gain, shift):
    centered = values - lax.optimization_barrier(jnp.mean(values, axis=-1, keepdims=True))
    spread = lax.optimization_barrier(jnp.mean(centered * centered, axis=-1, keepdims=True))
    return centered * lax.rsqrt(spread + epsilon) * gain + shift

def row_attention(operands):
    row_query, row_keyval, row_segment = operands
    key_part = row_keyval[:, :HD]
    value_part = row_keyval[:, HD:]
    scores = jnp.einsum('leh,kh->elk', row_query, key_part, precision=HIGHEST) * HD ** (-0.5)
    matches = row_segment[:, None] == row_segment[None, :]
    scores = low_back(jnp.where(matches[None], scores, neg_large))
    highest = lax.optimization_barrier(jnp.max(scores, axis=-1, keepdims=True))
    numerator = jnp.exp(scores - highest)
    probs = numerator / lax.optimization_barrier(jnp.sum(numerator, axis=-1, keepdims=True))
    context = jnp.einsum('elk,kh->leh', low(probs), value_part, precision=HIGHEST)
    return low_back(context)

def layer_block(params, inputs, expert_index, segments):
    ln1_gain, ln1_bias, w_router, w_query, b_query, w_keyval, w_out, b_out, ln2_gain, ln2_bias, w_up, b_up, w_down, b_down = params
    row_count = inputs.shape[0]
    normed = low(normalize(inputs, ln1_gain, ln1_bias))
    logits = low_back(jnp.einsum('bld,de->ble', normed, w_router, precision=HIGHEST))
    experts_range = jnp.arange(EXPERTS, dtype=jnp.int32)
    chosen = lax.optimization_barrier(jnp.sum((expert_index[..., None] == experts_range).astype(jnp.float32), axis=2))
    shifted = jnp.exp(logits - lax.optimization_barrier(jnp.max(logits, axis=-1, keepdims=True))) * chosen
    gates = shifted / lax.optimization_barrier(jnp.sum(shifted, axis=-1, keepdims=True))
    queries = low_back(low(jnp.einsum('bld,df->blf', normed, w_query, precision=HIGHEST) + b_query))
    keyval = low_back(low(jnp.einsum('bld,df->blf', normed, w_keyval, precision=HIGHEST)))
    queries = queries.reshape(row_count, SEQ_LEN, EXPERTS, HD)
    context = lax.map(jax.checkpoint(row_attention), (queries, keyval, segments))
    mixed = low(gates[..., None] * context).reshape(row_count, SEQ_LEN, EXPERTS * HD)
    attended = low_back(jnp.einsum('blf,fd->bld', mixed, w_out, precision=HIGHEST) + b_out)
    middle = inputs + attended
    normed_two = low(normalize(middle, ln2_gain, ln2_bias))
    hidden = low_back(jnp.einsum('bld,df->blf', normed_two, w_up, precision=HIGHEST) + b_up)
    active = low(jax.nn.gelu(hidden))
    branch = low_back(jnp.einsum('blf,fd->bld', active, w_down, precision=HIGHEST) + b_down)
    return middle + branch

def reference(tokens, cotangent, expert_index, segments, ln1_gain, ln1_bias, w_router, w_query, b_query, w_keyval, w_out, b_out, ln2_gain, ln2_bias, w_up, b_up, w_down, b_down):
    params = (ln1_gain.astype(jnp.float32), ln1_bias.astype(jnp.float32), w_router.astype(jnp.float32), w_query.astype(jnp.float32), b_query.astype(jnp.float32), w_keyval.astype(jnp.float32), w_out.astype(jnp.float32), b_out.astype(jnp.float32), ln2_gain.astype(jnp.float32), ln2_bias.astype(jnp.float32), w_up.astype(jnp.float32), b_up.astype(jnp.float32), w_down.astype(jnp.float32), b_down.astype(jnp.float32))
    groups = ROWS // ROWS_DEV
    block_in = tokens.astype(jnp.float32).reshape(groups, ROWS_DEV, SEQ_LEN, D)
    block_cot = cotangent.astype(jnp.float32).reshape(groups, ROWS_DEV, SEQ_LEN, D)
    block_index = expert_index.reshape(groups, ROWS_DEV, SEQ_LEN, TOPK)
    block_seg = segments.reshape(groups, ROWS_DEV, SEQ_LEN)

    def step(totals, operands):
        rows_in, rows_cot, rows_index, rows_seg = operands

        def forward(weights_in, inputs_in):
            return layer_block(weights_in, inputs_in, rows_index, rows_seg)
        result, puller = jax.vjp(forward, params, rows_in)
        grad_params, grad_inputs = puller(rows_cot)
        totals = jax.tree.map(jnp.add, totals, grad_params)
        return (totals, (result.astype(jnp.bfloat16), grad_inputs.astype(jnp.bfloat16)))
    zeros = jax.tree.map(jnp.zeros_like, params)
    totals, (results, grad_rows) = lax.scan(step, zeros, (block_in, block_cot, block_index, block_seg))
    return (results.reshape(ROWS, SEQ_LEN, D), grad_rows.reshape(ROWS, SEQ_LEN, D), totals[0], totals[1], totals[2], totals[3], totals[4], totals[5], totals[6], totals[7], totals[8], totals[9], totals[10], totals[11], totals[12], totals[13])
```

```python
import functools

import jax
import jax.numpy as jnp
from jax import lax
from jax.experimental import pallas as pl
from jax.experimental.pallas import tpu as pltpu
from jax.sharding import PartitionSpec as P

EPS = 1e-05
NEG = -1e30
C0 = 0.7978845608028654
C1 = 0.7978845608028654 * 0.044715
PARTS = (8,)
R = 2
VMEM_LIMIT = 60 * 1024 * 1024
F32 = jnp.float32
BF16 = jnp.bfloat16


def mm(a, b):
    return lax.dot_general(a, b, (((1,), (0,)), ((), ())), preferred_element_type=F32)


def mmt(a, b):
    return lax.dot_general(a, b, (((1,), (1,)), ((), ())), preferred_element_type=F32)


def fold8(v):
    return jnp.sum(v.reshape(v.shape[0] // 8, 8, v.shape[1]), axis=0)


def norm_parts(x):
    mean = jnp.mean(x, axis=-1, keepdims=True)
    xc = x - mean
    rstd = lax.rsqrt(jnp.mean(xc * xc, axis=-1, keepdims=True) + EPS)
    return xc * rstd, rstd


def norm_back(d, xhat, rstd):
    return rstd * (
        d
        - jnp.mean(d, axis=-1, keepdims=True)
        - xhat * jnp.mean(d * xhat, axis=-1, keepdims=True)
    )


def rel(bits, v):
    j = 0
    for src, dst in bits:
        j = j | (((v >> src) & 1) << dst)
    return j


def spread_matrix():
    m = lax.broadcasted_iota(jnp.int32, (128, 512), 0)
    lane = lax.broadcasted_iota(jnp.int32, (128, 512), 1)
    return jnp.where(m == (lane >> 6) * 16 + (lane & 15), 1.0, 0.0).astype(BF16)


def spread_rows():
    row = lax.broadcasted_iota(jnp.int32, (16, 512), 0)
    lane = lax.broadcasted_iota(jnp.int32, (16, 512), 1)
    return ((lane >> 4) & 3) + 8 == row


def kernel_a(bits, nblk, parts, sc, pack, tok, can, vec, bup, *kvs):
    me = sc[0]
    for b in range(nblk):
        can[b * 16 : (b + 1) * 16, :] = pack[rel(bits, me ^ b)]
    turned = jnp.transpose(can[:, 640:768].astype(F32))
    rows = turned[8:24]
    vec[...] = rows
    ex = spread_matrix()
    pick = spread_rows()
    width = can.shape[0]
    for b in range(4):
        wide = mm(rows[:, b * 128 : (b + 1) * 128].astype(BF16), ex)
        line = jnp.sum(jnp.where(pick, wide, 0.0), axis=0, keepdims=True)
        bup[:, b * width : (b + 1) * width] = jnp.broadcast_to(line, (8, width))
    gain = vec[0:1, :]
    shift = vec[1:2, :]
    row = 0
    for kv, count in zip(kvs, parts):
        for r in range(count):
            xhat, unused = norm_parts(tok[row].astype(F32))
            normed = (xhat * gain + shift).astype(BF16)
            kv[r] = mm(normed, can[:, 512:640]).astype(BF16)
            row += 1


def kernel_b(cfg, *refs):
    first, last, steps, bits_u, bits_d, gbits_u, gbits_d, nblk, nseq = cfg
    refs = list(refs)

    def take(n):
        got = refs[:n]
        del refs[:n]
        return got

    sc, tok, cot, idx, seg = take(5)
    kvs = take(nseq)
    can, vec, bup = take(3)
    u_own, u_got, d_own, d_got = take(4)
    acc_in = []
    if not first:
        acc_in = take(6)
        take(2)
    out_ref, part_ref = take(2)
    dkvs = take(nseq)
    (vacc,) = take(1)
    if last:
        gu_ref, gd_ref = take(2)
        acc_up, acc_dn, acc_wo, acc_wq, acc_r = take(5)
    else:
        acc_up, acc_dn, acc_wo, acc_wq, acc_r = take(5)
    (
        wup,
        wdn,
        wo,
        xn,
        q_s,
        qp,
        dp,
        idx_b,
        gate_b,
        cd,
        inner,
        prob,
        score,
        wide1,
        wide2,
        mid,
        xh2,
        rs2,
        n2,
        mix,
        hid,
        gac,
        act,
        ghd,
        low1,
        gl,
        wsem,
        asem,
    ) = refs

    me = sc[0]
    place = sc[1]
    step = pl.program_id(0)
    tile = tok.shape[0]
    local = tile // R
    ch = 64
    nch = tile // ch
    lane128 = lax.broadcasted_iota(jnp.int32, (ch, 128), 1)
    upper = lane128 >= 64
    half = lane128 >> 6
    accs = (acc_up, acc_dn, acc_wo, acc_wq, acc_r, vacc)

    @pl.when(step == 0)
    def _():
        for piece, base in ((u_own, 0), (u_got, u_own.shape[0])):
            for c in range(piece.shape[0]):
                blk = me ^ sum(((base + c) >> dst & 1) << src for src, dst in bits_u)
                pltpu.make_async_copy(
                    piece.at[c], wup.at[pl.ds(pl.multiple_of(blk * 16, 16), 16), :], wsem.at[0]
                ).start()
        for piece, base in ((d_own, 0), (d_got, d_own.shape[0])):
            for c in range(piece.shape[0]):
                blk = me ^ sum(((base + c) >> dst & 1) << src for src, dst in bits_d)
                pltpu.make_async_copy(
                    piece.at[c, pl.ds(0, 64), :],
                    wdn.at[pl.ds(pl.multiple_of(blk * 64, 64), 64), :],
                    wsem.at[1],
                ).start()
                pltpu.make_async_copy(
                    piece.at[c, pl.ds(64, 16), :],
                    wo.at[pl.ds(pl.multiple_of(blk * 16, 16), 16), :],
                    wsem.at[2],
                ).start()
        if first:
            for a in accs:
                a[...] = jnp.zeros_like(a)
        else:
            for n, a in enumerate(accs):
                pltpu.make_async_copy(acc_in[n], a, asem.at[n]).start()

    gain1 = vec[0:1, :]
    shift1 = vec[1:2, :]
    bias_q = vec[2:3, :]
    bias_o = vec[3:4, :]
    gain2 = vec[4:5, :]
    shift2 = vec[5:6, :]
    bias_d = vec[6:7, :]

    def norm_chunk(c, carry):
        sl = pl.ds(pl.multiple_of(c * ch, ch), ch)
        xhat, unused = norm_parts(tok[sl, :].astype(F32))
        xn[sl, :] = (xhat * gain1 + shift1).astype(BF16)
        return carry

    lax.fori_loop(0, nch, norm_chunk, 0)
    q_s[...] = mm(xn[...], can[:, 0:512])
    low1[...] = mm(xn[...], can[:, 640:768])
    for r in range(R):
        for s in range(2):
            line = idx[r, s : s + 1, :].astype(F32)
            idx_b[s, r * local : (r + 1) * local, :] = jnp.transpose(
                jnp.broadcast_to(line, (128, local))
            ).astype(jnp.int32)

    def gate_chunk(c, carry):
        sl = pl.ds(pl.multiple_of(c * ch, ch), ch)
        logits = low1[sl, :]
        i0 = idx_b[0, sl, :]
        i1 = idx_b[1, sl, :]
        top = jnp.max(jnp.where(lane128 < 8, logits, -jnp.inf), axis=-1, keepdims=True)
        e0 = jnp.exp(jnp.sum(jnp.where(lane128 == i0, logits, 0.0), axis=-1, keepdims=True) - top)
        e1 = jnp.exp(jnp.sum(jnp.where(lane128 == i1, logits, 0.0), axis=-1, keepdims=True) - top)
        total = e0 + e1
        gate_b[0, sl, :] = jnp.broadcast_to(e0 / total, (ch, 128))
        gate_b[1, sl, :] = jnp.broadcast_to(e1 / total, (ch, 128))
        r = c // (local // ch)
        at = pl.multiple_of((c % (local // ch)) * ch, ch)
        f0 = jnp.zeros((ch, 128), F32)
        f1 = jnp.zeros((ch, 128), F32)
        for b in range(4):
            q = (q_s[sl, b * 128 : (b + 1) * 128] + bias_q[:, b * 128 : (b + 1) * 128]) * 0.125
            f0 = f0 + jnp.where(half + 2 * b == i0, q, 0.0)
            f1 = f1 + jnp.where(half + 2 * b == i1, q, 0.0)
        f0 = f0 + pltpu.roll(f0, 64, 1)
        f1 = f1 + pltpu.roll(f1, 64, 1)
        qp[r, pl.ds(at, ch), :] = jnp.where(upper, 0.0, f0).astype(BF16)
        qp[r, pl.ds(local + at, ch), :] = jnp.where(upper, 0.0, f1).astype(BF16)
        return carry

    lax.fori_loop(0, nch, gate_chunk, 0)

    for r in range(R):
        for m in range(nseq):
            score[:, m * local : (m + 1) * local] = mmt(qp[r], kvs[m][r])
        seg_k = jnp.concatenate(
            [
                seg[r, :, pl.ds(pl.multiple_of((place ^ m) * local, 128), local)]
                for m in range(nseq)
            ],
            axis=1,
        )
        own = seg[r, :, pl.ds(pl.multiple_of(place * local, 128), local)].astype(F32)
        inner[0:local, :] = jnp.transpose(jnp.broadcast_to(own, (128, local)))

        def soft_chunk(c, carry, r=r, seg_k=seg_k):
            at = pl.multiple_of(c * 16, 16)
            match = inner[pl.ds(at, 16), 0:1].astype(jnp.int32) == seg_k
            for s in range(2):
                sl = pl.ds(pl.multiple_of(s * local + at, 16), 16)
                sc_ = jnp.where(match, score[sl, :], NEG)
                num = jnp.exp(sc_ - jnp.max(sc_, axis=-1, keepdims=True))
                total = jnp.sum(num, axis=-1, keepdims=True)
                prob[r, sl, :] = (num / total).astype(BF16)
            return carry

        lax.fori_loop(0, local // 16, soft_chunk, 0, unroll=2)
        ctx = jnp.zeros((2 * local, 128), F32)
        for m in range(nseq):
            ctx = ctx + mm(prob[r, :, m * local : (m + 1) * local], kvs[m][r])
        up2 = lax.broadcasted_iota(jnp.int32, ctx.shape, 1) >= 64
        ctx = jnp.where(up2, ctx, 0.0)
        ctx = ctx + pltpu.roll(ctx, 64, 1)
        cd[0, r * local : (r + 1) * local, :] = ctx[:local]
        cd[1, r * local : (r + 1) * local, :] = ctx[local:]

    @pl.when(step == 0)
    def _():
        for n, w in enumerate((wup, wdn, wo)):
            pltpu.make_async_copy(w, w, wsem.at[n]).wait()
        if not first:
            for n, a in enumerate(accs):
                pltpu.make_async_copy(acc_in[n], a, asem.at[n]).wait()

    def mix_chunk(c, carry):
        sl = pl.ds(pl.multiple_of(c * ch, ch), ch)
        i0 = idx_b[0, sl, :]
        i1 = idx_b[1, sl, :]
        m0 = gate_b[0, sl, :] * cd[0, sl, :]
        m1 = gate_b[1, sl, :] * cd[1, sl, :]
        for b in range(4):
            mix[sl, b * 128 : (b + 1) * 128] = jnp.where(
                half + 2 * b == i0, m0, jnp.where(half + 2 * b == i1, m1, 0.0)
            ).astype(BF16)
        return carry

    lax.fori_loop(0, nch, mix_chunk, 0)
    wide1[...] = mm(mix[...], wo[...])

    def mid_chunk(c, carry):
        sl = pl.ds(pl.multiple_of(c * ch, ch), ch)
        middle = tok[sl, :].astype(F32) + (wide1[sl, :] + bias_o)
        mid[sl, :] = middle
        xhat, rstd = norm_parts(middle)
        xh2[sl, :] = xhat
        rs2[sl, :] = jnp.broadcast_to(rstd, (ch, 128))
        n2[sl, :] = (xhat * gain2 + shift2).astype(BF16)
        return carry

    lax.fori_loop(0, nch, mid_chunk, 0)

    n2_t = jnp.transpose(n2[...])
    cot_t = jnp.transpose(cot[...])
    width = hid.shape[2]
    for j in range(wup.shape[1] // width):
        k = j % 2
        js = slice(j * width, (j + 1) * width)
        hid[k] = mm(n2[...], wup[:, js])
        gac[k] = mmt(cot[...], wdn[js, :])
        bias = bup[0:1, js]
        total = jnp.zeros((8, width), F32)
        for c in range(tile // 32):
            sl = slice(c * 32, (c + 1) * 32)
            h = hid[k, sl, :] + bias
            h2 = h * h
            t = jnp.tanh(h * (C0 + C1 * h2))
            hh = 0.5 * h
            act[k, sl, :] = (hh + hh * t).astype(BF16)
            slope = (0.5 + 0.5 * t) + hh * (1.0 - t * t) * (C0 + (3.0 * C1) * h2)
            g = (gac[k, sl, :] * slope).astype(BF16)
            ghd[k, sl, :] = g
            total = total + fold8(g.astype(F32))
        vacc[(7 + j) * 8 : (8 + j) * 8, :] += total
        o = mm(act[k], wdn[js, :])
        g2 = mmt(ghd[k], wup[:, js])
        if j == 0:
            wide1[...] = o
            wide2[...] = g2
        else:
            wide1[...] += o
            wide2[...] += g2
        acc_up[:, js] += mm(n2_t, ghd[k])
        acc_dn[:, js] += mm(cot_t, act[k])

    def out_chunk(c, carry):
        sl = pl.ds(pl.multiple_of(c * ch, ch), ch)
        out_ref[sl, :] = (mid[sl, :] + (wide1[sl, :] + bias_d)).astype(BF16)
        ct = cot[sl, :].astype(F32)
        g = wide2[sl, :]
        xhat = xh2[sl, :]
        gm = ct + norm_back(g * gain2, xhat, rs2[sl, 0:1])
        mid[sl, :] = gm
        low = gm.astype(BF16)
        n2[sl, :] = low
        vacc[24:32, :] += fold8(low.astype(F32))
        vacc[32:40, :] += fold8(g * xhat)
        vacc[40:48, :] += fold8(g)
        vacc[48:56, :] += fold8(ct)
        return carry

    lax.fori_loop(0, nch, out_chunk, 0)

    acc_wo[...] += mm(jnp.transpose(mix[...]), n2[...])
    wide1[...] = mmt(n2[...], wo[...])

    def gate_back_chunk(c, carry):
        sl = pl.ds(pl.multiple_of(c * ch, ch), ch)
        i0 = idx_b[0, sl, :]
        i1 = idx_b[1, sl, :]
        f0 = jnp.zeros((ch, 128), F32)
        f1 = jnp.zeros((ch, 128), F32)
        for b in range(4):
            g = wide1[sl, b * 128 : (b + 1) * 128]
            f0 = f0 + jnp.where(half + 2 * b == i0, g, 0.0)
            f1 = f1 + jnp.where(half + 2 * b == i1, g, 0.0)
        f0 = jnp.where(upper, f0 + pltpu.roll(f0, 64, 1), 0.0)
        f1 = jnp.where(upper, f1 + pltpu.roll(f1, 64, 1), 0.0)
        c0 = cd[0, sl, :]
        c1 = cd[1, sl, :]
        g0 = gate_b[0, sl, :]
        g1 = gate_b[1, sl, :]
        gg0 = jnp.sum(f0 * c0, axis=-1, keepdims=True)
        gg1 = jnp.sum(f1 * c1, axis=-1, keepdims=True)
        both = g0 * gg0 + g1 * gg1
        gl[sl, :] = jnp.where(
            lane128 == i0, g0 * (gg0 - both), jnp.where(lane128 == i1, g1 * (gg1 - both), 0.0)
        ).astype(BF16)
        d0 = (g0 * f0).astype(BF16)
        d1 = (g1 * f1).astype(BF16)
        r = c // (local // ch)
        at = pl.multiple_of((c % (local // ch)) * ch, ch)
        s0 = pl.ds(r * 2 * local + at, ch)
        s1 = pl.ds(r * 2 * local + local + at, ch)
        dp[r, pl.ds(at, ch), :] = d0
        dp[r, pl.ds(local + at, ch), :] = d1
        inner[s0, :] = jnp.broadcast_to(
            jnp.sum(d0.astype(F32) * c0, axis=-1, keepdims=True), (ch, 128)
        )
        inner[s1, :] = jnp.broadcast_to(
            jnp.sum(d1.astype(F32) * c1, axis=-1, keepdims=True), (ch, 128)
        )
        return carry

    lax.fori_loop(0, nch, gate_back_chunk, 0)

    for r in range(R):
        for m in range(nseq):
            score[:, m * local : (m + 1) * local] = mmt(dp[r], kvs[m][r])
        dsc = act

        def score_chunk(c, carry, r=r):
            at = pl.multiple_of(c * 16, 16)
            sl = pl.ds(at, 16)
            inn = inner[pl.ds(pl.multiple_of(r * 2 * local + at, 16), 16), 0:1]
            for k in range(2):
                ks = slice(k * width, (k + 1) * width)
                dsc[k, sl, :] = (prob[r, sl, ks].astype(F32) * (score[sl, ks] - inn)).astype(BF16)
            return carry

        lax.fori_loop(0, 2 * local // 16, score_chunk, 0, unroll=2)
        q_t = jnp.transpose(qp[r])
        d_t = jnp.transpose(dp[r])
        dq = jnp.zeros((2 * local, 128), F32)
        for m in range(nseq):
            k = m * local // width
            ks = slice(m * local - k * width, m * local - k * width + local)
            ds_m = dsc[k, :, ks]
            dq = dq + mm(ds_m, kvs[m][r])
            dkv_t = mm(q_t, ds_m) + mm(d_t, prob[r, :, m * local : (m + 1) * local])
            dkvs[m][r] = jnp.transpose(dkv_t).astype(BF16)
        up2 = lax.broadcasted_iota(jnp.int32, dq.shape, 1) >= 64
        dq = jnp.where(up2, 0.0, dq) * 0.125
        dq = dq + pltpu.roll(dq, 64, 1)
        cd[0, r * local : (r + 1) * local, :] = dq[:local]
        cd[1, r * local : (r + 1) * local, :] = dq[local:]

    def query_chunk(c, carry):
        sl = pl.ds(pl.multiple_of(c * ch, ch), ch)
        i0 = idx_b[0, sl, :]
        i1 = idx_b[1, sl, :]
        m0 = cd[0, sl, :]
        m1 = cd[1, sl, :]
        for b in range(4):
            low = jnp.where(
                half + 2 * b == i0, m0, jnp.where(half + 2 * b == i1, m1, 0.0)
            ).astype(BF16)
            mix[sl, b * 128 : (b + 1) * 128] = low
            vacc[16:24, b * 128 : (b + 1) * 128] += fold8(low.astype(F32))
        return carry

    lax.fori_loop(0, nch, query_chunk, 0)
    xn_t = jnp.transpose(xn[...])
    acc_wq[...] += mm(xn_t, mix[...])
    acc_r[...] += mm(xn_t, gl[...])
    wide1[...] = mmt(mix[...], can[:, 0:512]) + mmt(gl[...], can[:, 640:768])

    def part_chunk(c, carry):
        sl = pl.ds(pl.multiple_of(c * ch, ch), ch)
        xhat, rstd = norm_parts(tok[sl, :].astype(F32))
        g = wide1[sl, :]
        part_ref[sl, :] = mid[sl, :] + norm_back(g * gain1, xhat, rstd)
        vacc[0:8, :] += fold8(g * xhat)
        vacc[8:16, :] += fold8(g)
        return carry

    lax.fori_loop(0, nch, part_chunk, 0)

    if last:

        @pl.when(step == steps - 1)
        def _():
            for b in range(nblk):
                j = rel(gbits_u, me ^ b)
                rows = slice(b * 16, (b + 1) * 16)
                gu_ref[j, :, 0:2048] = acc_up[rows, :].astype(BF16)
                gu_ref[j, :, 2048:2176] = acc_r[rows, :].astype(BF16)
                j = rel(gbits_d, me ^ b)
                gd_ref[j, 64:80, :] = acc_wo[rows, :].astype(BF16)
                gd_ref[j, 80:96, :] = acc_wq[rows, :].astype(BF16)
            for c in range(nblk // 2):
                both = jnp.transpose(acc_dn[:, c * 128 : (c + 1) * 128]).astype(BF16)
                gd_ref[rel(gbits_d, me ^ (2 * c)), 0:64, :] = both[:64]
                gd_ref[rel(gbits_d, me ^ (2 * c + 1)), 0:64, :] = both[64:]


def kernel_e(cfg, *refs):
    first, last, steps, gbits, nblk, nseq = cfg
    refs = list(refs)

    def take(n):
        got = refs[:n]
        del refs[:n]
        return got

    sc, part, tok = take(3)
    dkvs = take(nseq)
    can, vec, vacc = take(3)
    acc_in = []
    if not first:
        acc_in = take(2)
        take(1)
    (out_ref,) = take(1)
    if last:
        (gs_ref,) = take(1)
    acc_kv, acc_l = take(2)
    wide, xh, xn, dk = refs
    me = sc[0]
    step = pl.program_id(0)
    tile = tok.shape[0]
    local = tile // R
    ch = 64
    nch = tile // ch
    gain = vec[0:1, :]
    shift = vec[1:2, :]

    @pl.when(step == 0)
    def _():
        if first:
            acc_kv[...] = jnp.zeros_like(acc_kv)
            acc_l[...] = jnp.zeros_like(acc_l)
        else:
            acc_kv[...] = acc_in[0][...]
            acc_l[...] = acc_in[1][...]

    for r in range(R):
        total = dkvs[0][r].astype(F32)
        for m in range(1, nseq):
            total = total + dkvs[m][r].astype(F32)
        dk[r * local : (r + 1) * local, :] = total.astype(BF16)
    wide[...] = mmt(dk[...], can[:, 512:640])

    def chunk(c, carry):
        sl = pl.ds(pl.multiple_of(c * ch, ch), ch)
        xhat, rstd = norm_parts(tok[sl, :].astype(F32))
        xn[sl, :] = (xhat * gain + shift).astype(BF16)
        g = wide[sl, :]
        out_ref[sl, :] = (part[sl, :] + norm_back(g * gain, xhat, rstd)).astype(BF16)
        acc_l[0:8, :] += fold8(g * xhat)
        acc_l[8:16, :] += fold8(g)
        return carry

    lax.fori_loop(0, nch, chunk, 0)
    acc_kv[...] += mm(jnp.transpose(xn[...]), dk[...])

    if last:

        @pl.when(step == steps - 1)
        def _():
            row = lax.broadcasted_iota(jnp.int32, (16, 512), 0)
            table = jnp.zeros((16, 512), F32)
            for v in range(7):
                line = vacc[v * 8 : (v + 1) * 8, :]
                if v < 2:
                    line = line + acc_l[v * 8 : (v + 1) * 8, :]
                table = jnp.where(row == v, jnp.sum(line, axis=0, keepdims=True), table)
            ex = spread_matrix()
            pick = spread_rows()
            ups = []
            for b in range(4):
                line = jnp.sum(vacc[(7 + b) * 8 : (8 + b) * 8, :], axis=0, keepdims=True)
                ups.append(mmt(jnp.where(pick, line, 0.0).astype(BF16), ex))
            table = table + jnp.concatenate(ups, axis=1)
            table = jnp.concatenate([table, jnp.zeros((112, 512), F32)], axis=0)
            cols = jnp.transpose(table)
            for b in range(nblk):
                j = rel(gbits, me ^ b)
                rows = slice(b * 16, (b + 1) * 16)
                gs_ref[j, :, 0:128] = acc_kv[rows, :].astype(BF16)
                gs_ref[j, :, 128:256] = cols[rows, :].astype(BF16)


def swap(x, hop, sizes):
    axis, mask = hop
    return lax.ppermute(x, axis, [(i, i ^ mask) for i in range(sizes[axis])])


def widen(x, order, sizes):
    for hop in order[:-1]:
        x = jnp.concatenate([x, swap(x, hop, sizes)], axis=0)
    return x, swap(x, order[-1], sizes)


def narrow(x, order, sizes):
    for n, hop in enumerate(order):
        h = x.shape[0] // 2
        got = swap(x[h:], hop, sizes)
        x = x[:h].astype(F32) + got.astype(F32)
        if n < len(order) - 1:
            x = x.astype(BF16)
    return x[0]


def whole(shape):
    zeros = (0,) * len(shape)
    return pl.BlockSpec(shape, lambda i: zeros, pipeline_mode=pl.Buffered(1))


def body(
    sizes,
    tokens,
    cotangent,
    expert_index,
    segments,
    ln1_gain,
    ln1_bias,
    w_router,
    w_query,
    b_query,
    w_keyval,
    w_out,
    b_out,
    ln2_gain,
    ln2_bias,
    w_up,
    b_up,
    w_down,
    b_down,
):
    nseq, nbatch = sizes["seq"], sizes["batch"]
    rows_dev, local, d = tokens.shape
    ff = w_up.shape[1]
    experts = w_router.shape[1]
    group = max(1, 16 // w_query.shape[0])
    high = nbatch // group
    nblk = nseq * high
    bidx = lax.axis_index("batch")
    sidx = lax.axis_index("seq")
    blk = sidx * high + bidx // group
    sc = jnp.stack([blk, sidx]).astype(jnp.int32)

    groups = [[g * group + i for i in range(group)] for g in range(high)]

    def near(w):
        if group == 1:
            return w
        return lax.all_gather(w, "batch", axis=0, tiled=True, axis_index_groups=groups)

    def near_sum(g):
        if group == 1:
            return g
        return lax.psum_scatter(
            g, "batch", scatter_dimension=0, tiled=True, axis_index_groups=groups
        )

    bb = [("batch", group << i) for i in range((high - 1).bit_length())]
    zz = [("seq", 1 << i) for i in range((nseq - 1).bit_length())]
    core, xy = bb[0], bb[1:]

    def bit_of(hop):
        axis, mask = hop
        step = mask // group if axis == "batch" else mask * high
        return step.bit_length() - 1

    def gather_bits(order):
        return tuple((bit_of(hop), i) for i, hop in enumerate(order))

    def scatter_bits(order):
        return tuple((bit_of(hop), len(order) - 1 - i) for i, hop in enumerate(order))

    def weave(a, b):
        out = []
        for i in range(max(len(a), len(b))):
            out += list(a[i : i + 1]) + list(b[i : i + 1])
        return out

    order_a = zz[::-1] + xy + [core]
    order_u = weave(zz[::-1], xy) + [core]
    order_d = weave(xy, zz[::-1]) + [core]
    back_u = [core] + xy[::-1] + zz
    back_d = [core] + xy + zz
    back_s = [core] + xy[::-1] + zz

    cols = [near(v)[:, None] for v in (ln1_gain, ln1_bias, b_query, b_out, ln2_gain, ln2_bias, b_down)]
    bu = jnp.transpose(near(b_up).reshape(-1, 16))
    pad0 = jnp.zeros((16, 1), BF16)
    pad1 = jnp.zeros((16, 128 - 20), BF16)
    pack = jnp.concatenate(
        [near(w_query), near(w_keyval), near(w_router)] + cols + [pad0, bu, pad1], axis=1
    )[None]
    own, got = widen(pack, order_a, sizes)
    pack = jnp.concatenate([own, got], axis=0)
    u_own, u_got = widen(near(w_up)[None], order_u, sizes)
    d_own, d_got = widen(
        jnp.concatenate([near(w_down), near(w_out)], axis=0)[None], order_d, sizes
    )

    smem = pl.BlockSpec(memory_space=pltpu.SMEM)
    anywhere = pl.BlockSpec(memory_space=pl.ANY)
    params = pltpu.CompilerParams(vmem_limit_bytes=VMEM_LIMIT)
    shape = jax.ShapeDtypeStruct

    can, vec, bup, *kv_parts = pl.pallas_call(
        functools.partial(kernel_a, gather_bits(order_a), nblk, PARTS),
        out_shape=(
            shape((d, 768), BF16),
            shape((16, d), F32),
            shape((8, ff), F32),
        )
        + tuple(shape((n, local, 128), BF16) for n in PARTS),
        in_specs=[smem, pl.BlockSpec(memory_space=pltpu.VMEM), pl.BlockSpec(memory_space=pltpu.VMEM)],
        out_specs=tuple(pl.BlockSpec(memory_space=pltpu.VMEM) for unused in range(3 + len(PARTS))),
        compiler_params=params,
        name="project",
    )(sc, pack, tokens)

    flat = (rows_dev * local, d)
    tok = tokens.reshape(flat)
    cot = cotangent.reshape(flat)
    idx = jnp.transpose(expert_index, (0, 2, 1))
    seg = segments[:, None, :]
    tile = R * local

    kv_all = [
        [kv] + [swap(kv, ("seq", m), sizes) for m in range(1, nseq)] for kv in kv_parts
    ]
    acc_shapes = (
        shape((d, ff), F32),
        shape((d, ff), F32),
        shape((d, d), F32),
        shape((d, d), F32),
        shape((d, 128), F32),
    )
    vacc_shape = shape((88, d), F32)
    row0 = 0
    acc = None
    out = part = vacc = None
    dkv_all = []
    for p, count in enumerate(PARTS):
        first, last = p == 0, p == len(PARTS) - 1
        steps = count // R
        base = row0 // R
        rowspec = pl.BlockSpec((tile, d), lambda i, base=base: (base + i, 0))
        kvspec = pl.BlockSpec((R, local, 128), lambda i: (i, 0, 0))
        ins = [sc, tok, cot, idx, seg] + kv_all[p] + [can, vec, bup, u_own, u_got, d_own, d_got]
        specs = [
            smem,
            rowspec,
            rowspec,
            pl.BlockSpec((R, 2, local), lambda i, base=base: (base + i, 0, 0)),
            pl.BlockSpec((R, 1, local * nseq), lambda i, base=base: (base + i, 0, 0)),
        ]
        specs += [kvspec] * nseq
        specs += [whole(can.shape), whole(vec.shape), whole(bup.shape)] + [anywhere] * 4
        alias = {}
        if not first:
            ins += list(acc) + [vacc, out, part]
            specs += [anywhere] * 8
            alias = {len(ins) - 2: 0, len(ins) - 1: 1}
        outs = [shape(flat, BF16), shape(flat, F32)]
        outs += [shape((count, local, 128), BF16)] * nseq + [vacc_shape]
        ospecs = [rowspec, rowspec] + [kvspec] * nseq + [whole(vacc_shape.shape)]
        scratch = []
        if last:
            outs += [shape((nblk, 16, ff + 128), BF16), shape((nblk, 96, d), BF16)]
            ospecs += [whole((nblk, 16, ff + 128)), whole((nblk, 96, d))]
            scratch += [pltpu.VMEM(a.shape, F32) for a in acc_shapes]
        else:
            outs += list(acc_shapes)
            ospecs += [whole(a.shape) for a in acc_shapes]
        wide = (tile, d)
        scratch += [
            pltpu.VMEM((d, ff), BF16),
            pltpu.VMEM((ff, d), BF16),
            pltpu.VMEM((d, d), BF16),
            pltpu.VMEM(wide, BF16),
            pltpu.VMEM(wide, F32),
            pltpu.VMEM((R, 2 * local, 128), BF16),
            pltpu.VMEM((R, 2 * local, 128), BF16),
            pltpu.VMEM((2, tile, 128), jnp.int32),
            pltpu.VMEM((2, tile, 128), F32),
            pltpu.VMEM((2, tile, 128), F32),
            pltpu.VMEM((2 * tile, 128), F32),
            pltpu.VMEM((R, 2 * local, nseq * local), BF16),
            pltpu.VMEM((2 * local, nseq * local), F32),
            pltpu.VMEM(wide, F32),
            pltpu.VMEM(wide, F32),
            pltpu.VMEM(wide, F32),
            pltpu.VMEM(wide, F32),
            pltpu.VMEM((tile, 128), F32),
            pltpu.VMEM(wide, BF16),
            pltpu.VMEM(wide, BF16),
            pltpu.VMEM((2, tile, 512), F32),
            pltpu.VMEM((2, tile, 512), F32),
            pltpu.VMEM((2, tile, 512), BF16),
            pltpu.VMEM((2, tile, 512), BF16),
            pltpu.VMEM((tile, 128), F32),
            pltpu.VMEM((tile, 128), BF16),
            pltpu.SemaphoreType.DMA((3,)),
            pltpu.SemaphoreType.DMA((6,)),
        ]
        cfg = (
            first,
            last,
            steps,
            gather_bits(order_u),
            gather_bits(order_d),
            scatter_bits(back_u),
            scatter_bits(back_d),
            nblk,
            nseq,
        )
        got = pl.pallas_call(
            functools.partial(kernel_b, cfg),
            grid=(steps,),
            out_shape=tuple(outs),
            in_specs=specs,
            out_specs=tuple(ospecs),
            scratch_shapes=scratch,
            input_output_aliases=alias,
            compiler_params=params,
            name="layer",
        )(*ins)
        out, part = got[0], got[1]
        dkv = got[2 : 2 + nseq]
        dkv_all.append(
            [dkv[0]] + [swap(dkv[m], ("seq", m), sizes) for m in range(1, nseq)]
        )
        vacc = got[2 + nseq]
        acc = got[3 + nseq :]
        row0 += count

    gu, gd = acc
    gu = narrow(gu, back_u, sizes)
    gd = narrow(gd, back_d, sizes)

    row0 = 0
    grad = None
    eacc = None
    for p, count in enumerate(PARTS):
        first, last = p == 0, p == len(PARTS) - 1
        steps = count // R
        base = row0 // R
        rowspec = pl.BlockSpec((tile, d), lambda i, base=base: (base + i, 0))
        kvspec = pl.BlockSpec((R, local, 128), lambda i: (i, 0, 0))
        ins = [sc, part, tok] + dkv_all[p] + [can, vec, vacc]
        specs = [smem, rowspec, rowspec] + [kvspec] * nseq
        specs += [whole(can.shape), whole(vec.shape), whole(vacc.shape)]
        alias = {}
        if not first:
            ins += list(eacc) + [grad]
            specs += [whole((d, 128)), whole((16, d)), anywhere]
            alias = {len(ins) - 1: 0}
        outs = [shape(flat, BF16)]
        ospecs = [rowspec]
        scratch = []
        if last:
            outs += [shape((nblk, 16, 256), BF16)]
            ospecs += [whole((nblk, 16, 256))]
            scratch += [pltpu.VMEM((d, 128), F32), pltpu.VMEM((16, d), F32)]
        else:
            outs += [shape((d, 128), F32), shape((16, d), F32)]
            ospecs += [whole((d, 128)), whole((16, d))]
        scratch += [
            pltpu.VMEM((tile, d), F32),
            pltpu.VMEM((8, 128), F32),
            pltpu.VMEM((tile, d), BF16),
            pltpu.VMEM((tile, 128), BF16),
        ]
        cfg = (first, last, steps, scatter_bits(back_s), nblk, nseq)
        got = pl.pallas_call(
            functools.partial(kernel_e, cfg),
            grid=(steps,),
            out_shape=tuple(outs),
            in_specs=specs,
            out_specs=tuple(ospecs),
            scratch_shapes=scratch,
            input_output_aliases=alias,
            compiler_params=params,
            name="finish",
        )(*ins)
        grad = got[0]
        eacc = got[1:]
        row0 += count
    gs = narrow(eacc[0], back_s, sizes)

    def vector(v):
        return near_sum(gs[:, 128 + v])

    grad_b_up = near_sum(jnp.transpose(gs[:, 136:140]).reshape(-1))
    return (
        out.reshape(tokens.shape),
        grad.reshape(tokens.shape),
        vector(0),
        vector(1),
        near_sum(gu[:, ff : ff + experts]),
        near_sum(gd[80:96]),
        vector(2),
        near_sum(gs[:, :128]),
        near_sum(gd[64:80]),
        vector(3),
        vector(4),
        vector(5),
        near_sum(gu[:, :ff]),
        grad_b_up,
        near_sum(gd[:64]),
        vector(6),
    )


def solution(mesh):
    sizes = {name: mesh.shape[name] for name in ("seq", "batch")}
    both = ("seq", "batch")
    row = P("batch", "seq", None)
    vector, matrix = P(both), P(both, None)
    in_specs = (
        row,
        row,
        row,
        P("batch", None),
        vector,
        vector,
        matrix,
        matrix,
        vector,
        matrix,
        matrix,
        vector,
        vector,
        vector,
        matrix,
        vector,
        matrix,
        vector,
    )
    out_specs = (
        row,
        row,
        vector,
        vector,
        matrix,
        matrix,
        vector,
        matrix,
        matrix,
        vector,
        vector,
        vector,
        matrix,
        vector,
        matrix,
        vector,
    )
    return jax.shard_map(
        functools.partial(body, sizes),
        mesh=mesh,
        in_specs=in_specs,
        out_specs=out_specs,
        check_vma=False,
    )
```

```python
import functools

import jax
import jax.numpy as jnp
from jax import lax
from jax.experimental import pallas as pl
from jax.experimental.pallas import tpu as pltpu
from jax.sharding import PartitionSpec as P

EPS = 1e-05
NEG = -1e30
C0 = 0.7978845608028654
C1 = 0.7978845608028654 * 0.044715
PARTS = (4, 4)
R = 2
FC = 32
FU = 4
RU = 2
CH = 32
UN = 16
SC = 64
SU = 4
SD = 64
SV = 4
VMEM_LIMIT = 60 * 1024 * 1024
F32 = jnp.float32
BF16 = jnp.bfloat16


def mm(a, b):
    return lax.dot_general(a, b, (((1,), (0,)), ((), ())), preferred_element_type=F32)


def mmt(a, b):
    return lax.dot_general(a, b, (((1,), (1,)), ((), ())), preferred_element_type=F32)


def fold8(v):
    return jnp.sum(v.reshape(v.shape[0] // 8, 8, v.shape[1]), axis=0)


def norm_parts(x):
    mean = jnp.mean(x, axis=-1, keepdims=True)
    xc = x - mean
    rstd = lax.rsqrt(jnp.mean(xc * xc, axis=-1, keepdims=True) + EPS)
    return xc * rstd, rstd


def norm_back(d, xhat, rstd):
    return rstd * (
        d
        - jnp.mean(d, axis=-1, keepdims=True)
        - xhat * jnp.mean(d * xhat, axis=-1, keepdims=True)
    )


def rel(bits, v):
    j = 0
    for src, dst in bits:
        j = j | (((v >> src) & 1) << dst)
    return j


def kernel_a(bits, nblk, parts, sc, own, got, tok, can, vec, bup, *kvs):
    *kvs, pack = kvs
    me = sc[0]
    pack[0 : nblk // 2] = own[...]
    pack[nblk // 2 :] = got[...]
    lane = lax.broadcasted_iota(jnp.int32, (16, 128), 1)
    for g in range(nblk // 8):
        rows = jnp.zeros((16, 128), F32)
        for i in range(8):
            b = g * 8 + i
            block = pack[rel(bits, me ^ b)]
            can[b * 16 : (b + 1) * 16, 0:640] = block[:, 0:640]
            tail = block[:, 640:768].astype(F32)
            rows = jnp.where(lane >> 4 == i, pltpu.roll(tail, i * 16, 1) if i else tail, rows)
            line = pltpu.roll(tail, 112 if i % 2 == 0 else 48, 1)
            wide = line if i % 2 == 0 else jnp.where(lane >= 64, line, wide)
            if i % 2:
                bup[:, (b // 2) * 128 : (b // 2 + 1) * 128] = wide[0:8]
        vec[:, g * 128 : (g + 1) * 128] = rows
    router = jnp.concatenate([vec[8:16, :], jnp.zeros((120, vec.shape[1]), F32)], axis=0)
    can[:, 640:768] = jnp.transpose(router).astype(BF16)
    gain = vec[0:1, :]
    shift = vec[1:2, :]
    row = 0
    for kv, count in zip(kvs, parts):
        for r in range(count):
            xhat, unused = norm_parts(tok[row].astype(F32))
            normed = (xhat * gain + shift).astype(BF16)
            kv[r] = mm(normed, can[:, 512:640]).astype(BF16)
            row += 1


def kernel_b(cfg, *refs):
    first, last, steps, bits_u, bits_d, gbits_u, gbits_d, nblk, nseq = cfg
    refs = list(refs)

    def take(n):
        got = refs[:n]
        del refs[:n]
        return got

    sc, tok, cot, idx, seg = take(5)
    kvs = take(nseq)
    can, vec, bup = take(3)
    u_own, u_got, d_own, d_got = take(4)
    acc_in = []
    if not first:
        acc_in = take(5)
        take(2)
    out_ref, part_ref = take(2)
    dkvs = take(nseq)
    (vacc,) = take(1)
    if last:
        gu_refs = take(2)
        gd_refs = take(2)
    acc_up, acc_dn, acc_wo, acc_wq = take(4)
    (
        wup,
        wdn,
        wo,
        xn,
        q_s,
        qp,
        dp,
        idx_b,
        gate_b,
        cd,
        inner,
        prob,
        score,
        wide1,
        wide2,
        mid,
        xh2,
        rs2,
        n2,
        mix,
        hid,
        gac,
        act,
        ghd,
        low1,
        gl,
        n2_t,
        cot_t,
        wsem,
        asem,
    ) = refs

    me = sc[0]
    place = sc[1]
    step = pl.program_id(0)
    tile = tok.shape[0]
    local = tile // R
    ch = CH
    nch = tile // ch
    lane128 = lax.broadcasted_iota(jnp.int32, (ch, 128), 1)
    upper = lane128 >= 64
    half = lane128 >> 6
    accs = (acc_up, acc_dn, acc_wo, acc_wq, vacc)

    @pl.when(step == 0)
    def _():
        for piece, base in ((u_own, 0), (u_got, u_own.shape[0])):
            for c in range(piece.shape[0]):
                blk = me ^ sum(((base + c) >> dst & 1) << src for src, dst in bits_u)
                pltpu.make_async_copy(
                    piece.at[c], wup.at[pl.ds(pl.multiple_of(blk * 16, 16), 16), :], wsem.at[0]
                ).start()
        for piece, base in ((d_own, 0), (d_got, d_own.shape[0])):
            for c in range(piece.shape[0]):
                blk = me ^ sum(((base + c) >> dst & 1) << src for src, dst in bits_d)
                pltpu.make_async_copy(
                    piece.at[c, pl.ds(0, 64), :],
                    wdn.at[pl.ds(pl.multiple_of(blk * 64, 64), 64), :],
                    wsem.at[1],
                ).start()
                pltpu.make_async_copy(
                    piece.at[c, pl.ds(64, 16), :],
                    wo.at[pl.ds(pl.multiple_of(blk * 16, 16), 16), :],
                    wsem.at[2],
                ).start()
        if first:
            for a in accs:
                a[...] = jnp.zeros_like(a)
        else:
            for n, a in enumerate(accs):
                pltpu.make_async_copy(acc_in[n], a, asem.at[n]).start()

    gain1 = vec[0:1, :]
    shift1 = vec[1:2, :]
    bias_q = vec[2:3, :]
    bias_o = vec[3:4, :]
    gain2 = vec[4:5, :]
    shift2 = vec[5:6, :]
    bias_d = vec[6:7, :]

    def norm_chunk(c, carry):
        sl = pl.ds(pl.multiple_of(c * ch, ch), ch)
        xhat, unused = norm_parts(tok[sl, :].astype(F32))
        xn[sl, :] = (xhat * gain1 + shift1).astype(BF16)
        return carry

    lax.fori_loop(0, nch, norm_chunk, 0, unroll=UN)
    q_s[...] = mm(xn[...], can[:, 0:512])
    low1[...] = mm(xn[...], can[:, 640:768])
    for r in range(R):
        for s in range(2):
            line = idx[r, s : s + 1, :].astype(F32)
            idx_b[s, r * local : (r + 1) * local, :] = jnp.transpose(
                jnp.broadcast_to(line, (128, local))
            ).astype(jnp.int32)

    def gate_chunk(c, carry):
        sl = pl.ds(pl.multiple_of(c * ch, ch), ch)
        logits = low1[sl, :]
        i0 = idx_b[0, sl, :]
        i1 = idx_b[1, sl, :]
        top = jnp.max(jnp.where(lane128 < 8, logits, -jnp.inf), axis=-1, keepdims=True)
        e0 = jnp.exp(jnp.sum(jnp.where(lane128 == i0, logits, 0.0), axis=-1, keepdims=True) - top)
        e1 = jnp.exp(jnp.sum(jnp.where(lane128 == i1, logits, 0.0), axis=-1, keepdims=True) - top)
        total = e0 + e1
        gate_b[0, sl, :] = jnp.broadcast_to(e0 / total, (ch, 128))
        gate_b[1, sl, :] = jnp.broadcast_to(e1 / total, (ch, 128))
        r = c // (local // ch)
        at = pl.multiple_of((c % (local // ch)) * ch, ch)
        f0 = jnp.zeros((ch, 128), F32)
        f1 = jnp.zeros((ch, 128), F32)
        for b in range(4):
            q = (q_s[sl, b * 128 : (b + 1) * 128] + bias_q[:, b * 128 : (b + 1) * 128]) * 0.125
            f0 = f0 + jnp.where(half + 2 * b == i0, q, 0.0)
            f1 = f1 + jnp.where(half + 2 * b == i1, q, 0.0)
        f0 = f0 + pltpu.roll(f0, 64, 1)
        f1 = f1 + pltpu.roll(f1, 64, 1)
        qp[r, pl.ds(at, ch), :] = jnp.where(upper, 0.0, f0).astype(BF16)
        qp[r, pl.ds(local + at, ch), :] = jnp.where(upper, 0.0, f1).astype(BF16)
        return carry

    lax.fori_loop(0, nch, gate_chunk, 0, unroll=UN)

    def attend(r, outer):
        for m in range(nseq):
            score[:, m * local : (m + 1) * local] = mmt(qp[r], kvs[m][r])
        seg_k = jnp.concatenate(
            [
                seg[r, :, pl.ds(pl.multiple_of((place ^ m) * local, 128), local)]
                for m in range(nseq)
            ],
            axis=1,
        )
        own = seg[r, :, pl.ds(pl.multiple_of(place * local, 128), local)].astype(F32)
        inner[0:local, :] = jnp.transpose(jnp.broadcast_to(own, (128, local)))

        def soft_chunk(c, carry):
            at = pl.multiple_of(c * SC, SC)
            match = inner[pl.ds(at, SC), 0:1].astype(jnp.int32) == seg_k
            for s in range(2):
                sl = pl.ds(pl.multiple_of(s * local + at, SC), SC)
                sc_ = jnp.where(match, score[sl, :], NEG)
                num = jnp.exp(sc_ - jnp.max(sc_, axis=-1, keepdims=True))
                total = jnp.sum(num, axis=-1, keepdims=True)
                prob[r, sl, :] = (num * (1.0 / total)).astype(BF16)
            return carry

        lax.fori_loop(0, local // SC, soft_chunk, 0, unroll=SU)
        ctx = jnp.zeros((2 * local, 128), F32)
        for m in range(nseq):
            ctx = ctx + mm(prob[r, :, m * local : (m + 1) * local], kvs[m][r])
        up2 = lax.broadcasted_iota(jnp.int32, ctx.shape, 1) >= 64
        ctx = jnp.where(up2, ctx, 0.0)
        ctx = ctx + pltpu.roll(ctx, 64, 1)
        own_rows = pl.ds(pl.multiple_of(r * local, local), local)
        cd[0, own_rows, :] = ctx[:local]
        cd[1, own_rows, :] = ctx[local:]
        return outer

    lax.fori_loop(0, R, attend, 0, unroll=RU)

    @pl.when(step == 0)
    def _():
        for n, w in enumerate((wup, wdn, wo)):
            pltpu.make_async_copy(w, w, wsem.at[n]).wait()
        if not first:
            for n, a in enumerate(accs):
                pltpu.make_async_copy(acc_in[n], a, asem.at[n]).wait()

    def mix_chunk(c, carry):
        sl = pl.ds(pl.multiple_of(c * ch, ch), ch)
        i0 = idx_b[0, sl, :]
        i1 = idx_b[1, sl, :]
        m0 = gate_b[0, sl, :] * cd[0, sl, :]
        m1 = gate_b[1, sl, :] * cd[1, sl, :]
        for b in range(4):
            mix[sl, b * 128 : (b + 1) * 128] = jnp.where(
                half + 2 * b == i0, m0, jnp.where(half + 2 * b == i1, m1, 0.0)
            ).astype(BF16)
        return carry

    lax.fori_loop(0, nch, mix_chunk, 0, unroll=UN)
    wide1[...] = mm(mix[...], wo[...])

    def mid_chunk(c, carry):
        sl = pl.ds(pl.multiple_of(c * ch, ch), ch)
        middle = tok[sl, :].astype(F32) + (wide1[sl, :] + bias_o)
        mid[sl, :] = middle
        xhat, rstd = norm_parts(middle)
        xh2[sl, :] = xhat
        rs2[sl, :] = jnp.broadcast_to(rstd, (ch, 128))
        n2[sl, :] = (xhat * gain2 + shift2).astype(BF16)
        return carry

    lax.fori_loop(0, nch, mid_chunk, 0, unroll=UN)

    n2_t[...] = jnp.transpose(n2[...])
    cot_t[...] = jnp.transpose(cot[...])
    width = hid.shape[2]
    wide1[...] = jnp.zeros_like(wide1)
    wide2[...] = jnp.zeros_like(wide2)

    def hidden_block(j, carry):
        js = pl.ds(pl.multiple_of(j * width, width), width)
        hid[0] = mm(n2[...], wup[:, js])
        gac[0] = mmt(cot[...], wdn[js, :])
        bias = bup[0:1, js]
        total = jnp.zeros((8, width), F32)
        for c in range(tile // FC):
            sl = slice(c * FC, (c + 1) * FC)
            h = hid[0, sl, :] + bias
            h2 = h * h
            t = jnp.tanh(h * (C0 + C1 * h2))
            hh = 0.5 * h
            act[0, sl, :] = (hh + hh * t).astype(BF16)
            slope = (0.5 + 0.5 * t) + hh * (1.0 - t * t) * (C0 + (3.0 * C1) * h2)
            g = (gac[0, sl, :] * slope).astype(BF16)
            ghd[0, sl, :] = g
            total = total + fold8(g.astype(F32))
        vacc[pl.ds(pl.multiple_of((7 + j) * 8, 8), 8), :] += total
        wide1[...] += mm(act[0], wdn[js, :])
        wide2[...] += mmt(ghd[0], wup[:, js])
        acc_up[:, js] += mm(n2_t[...], ghd[0])
        acc_dn[:, js] += mm(cot_t[...], act[0])
        return carry

    lax.fori_loop(0, wup.shape[1] // width, hidden_block, 0, unroll=FU)

    def out_chunk(c, carry):
        sl = pl.ds(pl.multiple_of(c * ch, ch), ch)
        out_ref[sl, :] = (mid[sl, :] + (wide1[sl, :] + bias_d)).astype(BF16)
        ct = cot[sl, :].astype(F32)
        g = wide2[sl, :]
        xhat = xh2[sl, :]
        gm = ct + norm_back(g * gain2, xhat, rs2[sl, 0:1])
        mid[sl, :] = gm
        low = gm.astype(BF16)
        n2[sl, :] = low
        vacc[24:32, :] += fold8(low.astype(F32))
        vacc[32:40, :] += fold8(g * xhat)
        vacc[40:48, :] += fold8(g)
        vacc[48:56, :] += fold8(ct)
        return carry

    lax.fori_loop(0, nch, out_chunk, 0, unroll=UN)

    acc_wo[...] += mm(jnp.transpose(mix[...]), n2[...])
    wide1[...] = mmt(n2[...], wo[...])

    def gate_back_chunk(c, carry):
        sl = pl.ds(pl.multiple_of(c * ch, ch), ch)
        i0 = idx_b[0, sl, :]
        i1 = idx_b[1, sl, :]
        f0 = jnp.zeros((ch, 128), F32)
        f1 = jnp.zeros((ch, 128), F32)
        for b in range(4):
            g = wide1[sl, b * 128 : (b + 1) * 128]
            f0 = f0 + jnp.where(half + 2 * b == i0, g, 0.0)
            f1 = f1 + jnp.where(half + 2 * b == i1, g, 0.0)
        f0 = jnp.where(upper, f0 + pltpu.roll(f0, 64, 1), 0.0)
        f1 = jnp.where(upper, f1 + pltpu.roll(f1, 64, 1), 0.0)
        c0 = cd[0, sl, :]
        c1 = cd[1, sl, :]
        g0 = gate_b[0, sl, :]
        g1 = gate_b[1, sl, :]
        gg0 = jnp.sum(f0 * c0, axis=-1, keepdims=True)
        gg1 = jnp.sum(f1 * c1, axis=-1, keepdims=True)
        both = g0 * gg0 + g1 * gg1
        gl[sl, :] = jnp.where(
            lane128 == i0, g0 * (gg0 - both), jnp.where(lane128 == i1, g1 * (gg1 - both), 0.0)
        ).astype(BF16)
        d0 = (g0 * f0).astype(BF16)
        d1 = (g1 * f1).astype(BF16)
        r = c // (local // ch)
        at = pl.multiple_of((c % (local // ch)) * ch, ch)
        s0 = pl.ds(r * 2 * local + at, ch)
        s1 = pl.ds(r * 2 * local + local + at, ch)
        dp[r, pl.ds(at, ch), :] = d0
        dp[r, pl.ds(local + at, ch), :] = d1
        inner[s0, :] = jnp.broadcast_to(
            jnp.sum(d0.astype(F32) * c0, axis=-1, keepdims=True), (ch, 128)
        )
        inner[s1, :] = jnp.broadcast_to(
            jnp.sum(d1.astype(F32) * c1, axis=-1, keepdims=True), (ch, 128)
        )
        return carry

    lax.fori_loop(0, nch, gate_back_chunk, 0, unroll=UN)

    width = hid.shape[2]

    def attend_back(r, outer):
        for m in range(nseq):
            score[:, m * local : (m + 1) * local] = mmt(dp[r], kvs[m][r])
        dsc = act

        def score_chunk(c, carry):
            at = pl.multiple_of(c * SD, SD)
            sl = pl.ds(at, SD)
            inn = inner[pl.ds(pl.multiple_of(r * 2 * local + at, SD), SD), 0:1]
            for k in range(2):
                ks = slice(k * width, (k + 1) * width)
                dsc[k, sl, :] = (prob[r, sl, ks].astype(F32) * (score[sl, ks] - inn)).astype(BF16)
            return carry

        lax.fori_loop(0, 2 * local // SD, score_chunk, 0, unroll=SV)
        q_t = jnp.transpose(qp[r])
        d_t = jnp.transpose(dp[r])
        dq = jnp.zeros((2 * local, 128), F32)
        for m in range(nseq):
            k = m * local // width
            ks = slice(m * local - k * width, m * local - k * width + local)
            ds_m = dsc[k, :, ks]
            dq = dq + mm(ds_m, kvs[m][r])
            dkv_t = mm(q_t, ds_m) + mm(d_t, prob[r, :, m * local : (m + 1) * local])
            dkvs[m][r] = jnp.transpose(dkv_t).astype(BF16)
        up2 = lax.broadcasted_iota(jnp.int32, dq.shape, 1) >= 64
        dq = jnp.where(up2, 0.0, dq) * 0.125
        dq = dq + pltpu.roll(dq, 64, 1)
        own_rows = pl.ds(pl.multiple_of(r * local, local), local)
        cd[0, own_rows, :] = dq[:local]
        cd[1, own_rows, :] = dq[local:]
        return outer

    lax.fori_loop(0, R, attend_back, 0, unroll=RU)

    def query_chunk(c, carry):
        sl = pl.ds(pl.multiple_of(c * ch, ch), ch)
        i0 = idx_b[0, sl, :]
        i1 = idx_b[1, sl, :]
        m0 = cd[0, sl, :]
        m1 = cd[1, sl, :]
        for b in range(4):
            low = jnp.where(
                half + 2 * b == i0, m0, jnp.where(half + 2 * b == i1, m1, 0.0)
            ).astype(BF16)
            mix[sl, b * 128 : (b + 1) * 128] = low
            vacc[16:24, b * 128 : (b + 1) * 128] += fold8(low.astype(F32))
        return carry

    lax.fori_loop(0, nch, query_chunk, 0, unroll=UN)
    xn_t = jnp.transpose(xn[...])
    acc_wq[...] += mm(xn_t, mix[...])
    vacc[88:104, :] += mm(jnp.transpose(gl[...])[0:16], xn[...])
    wide1[...] = mmt(mix[...], can[:, 0:512]) + mmt(gl[...], can[:, 640:768])

    def part_chunk(c, carry):
        sl = pl.ds(pl.multiple_of(c * ch, ch), ch)
        xhat, rstd = norm_parts(tok[sl, :].astype(F32))
        g = wide1[sl, :]
        part_ref[sl, :] = mid[sl, :] + norm_back(g * gain1, xhat, rstd)
        vacc[0:8, :] += fold8(g * xhat)
        vacc[8:16, :] += fold8(g)
        return carry

    lax.fori_loop(0, nch, part_chunk, 0, unroll=UN)

    if last:

        @pl.when(step == steps - 1)
        def _():
            for c in range(wdn.shape[0] // 128):
                cs = slice(c * 128, (c + 1) * 128)
                wdn[cs, :] = jnp.transpose(acc_dn[:, cs].astype(BF16))
            for j in range(nblk):
                h, i = j // (nblk // 2), j % (nblk // 2)
                b = me ^ sum((j >> dst & 1) << src for src, dst in gbits_u)
                rows = pl.ds(pl.multiple_of(b * 16, 16), 16)
                gu_refs[h][i, :, 0:2048] = acc_up[rows, :].astype(BF16)
                gu_refs[h][i, :, 2048:2560] = acc_wq[rows, :].astype(BF16)
                b = me ^ sum((j >> dst & 1) << src for src, dst in gbits_d)
                gd_refs[h][i, 0:64, :] = wdn[pl.ds(pl.multiple_of(b * 64, 64), 64), :]
                rows = pl.ds(pl.multiple_of(b * 16, 16), 16)
                gd_refs[h][i, 64:80, :] = acc_wo[rows, :].astype(BF16)


def kernel_e(cfg, *refs):
    first, last, steps, gbits, nblk, nseq = cfg
    refs = list(refs)

    def take(n):
        got = refs[:n]
        del refs[:n]
        return got

    sc, part, tok = take(3)
    dkvs = take(nseq)
    can, vec, vacc = take(3)
    acc_in = []
    if not first:
        acc_in = take(2)
        take(1)
    (out_ref,) = take(1)
    if last:
        gs_refs = take(2)
    acc_kv, acc_l = take(2)
    wide, xn, dk, small = refs
    me = sc[0]
    step = pl.program_id(0)
    tile = tok.shape[0]
    local = tile // R
    ch = CH
    nch = tile // ch
    gain = vec[0:1, :]
    shift = vec[1:2, :]

    @pl.when(step == 0)
    def _():
        if first:
            acc_kv[...] = jnp.zeros_like(acc_kv)
            acc_l[...] = jnp.zeros_like(acc_l)
        else:
            acc_kv[...] = acc_in[0][...]
            acc_l[...] = acc_in[1][...]

    for r in range(R):
        total = dkvs[0][r].astype(F32)
        for m in range(1, nseq):
            total = total + dkvs[m][r].astype(F32)
        dk[r * local : (r + 1) * local, :] = total.astype(BF16)
    wide[...] = mmt(dk[...], can[:, 512:640])

    def chunk(c, carry):
        sl = pl.ds(pl.multiple_of(c * ch, ch), ch)
        xhat, rstd = norm_parts(tok[sl, :].astype(F32))
        xn[sl, :] = (xhat * gain + shift).astype(BF16)
        g = wide[sl, :]
        out_ref[sl, :] = (part[sl, :] + norm_back(g * gain, xhat, rstd)).astype(BF16)
        acc_l[0:8, :] += fold8(g * xhat)
        acc_l[8:16, :] += fold8(g)
        return carry

    lax.fori_loop(0, nch, chunk, 0, unroll=UN)
    acc_kv[...] += mm(jnp.transpose(xn[...]), dk[...])

    if last:

        @pl.when(step == steps - 1)
        def _():
            row = lax.broadcasted_iota(jnp.int32, (16, 512), 0)
            table = jnp.zeros((16, 512), F32)
            for v in range(7):
                line = vacc[v * 8 : (v + 1) * 8, :]
                if v < 2:
                    line = line + acc_l[v * 8 : (v + 1) * 8, :]
                table = jnp.where(row == v, jnp.sum(line, axis=0, keepdims=True), table)
            router = vacc[88:104, :][0:8]
            table = table + jnp.concatenate([jnp.zeros((8, 512), F32), router], axis=0)
            ups = [
                jnp.sum(vacc[(7 + b) * 8 : (8 + b) * 8, :], axis=0, keepdims=True)
                for b in range(4)
            ]
            lane = lax.broadcasted_iota(jnp.int32, (16, 128), 1)
            first_row = lax.broadcasted_iota(jnp.int32, (16, 128), 0) == 0
            for b in range(nblk):
                g, i = b // 8, b % 8
                rows = table[:, g * 128 : (g + 1) * 128]
                if i:
                    rows = pltpu.roll(rows, 128 - i * 16, 1)
                c = b * 64 // 512
                at = (b * 64 % 512) // 128 * 128
                line = jnp.broadcast_to(ups[c][:, at : at + 128], (16, 128))
                line = pltpu.roll(line, 16 if b % 2 == 0 else 80, 1)
                tail = jnp.where(
                    lane < 16, rows, jnp.where(first_row & (lane < 80), line, 0.0)
                )
                small[b] = jnp.concatenate([acc_kv[b * 16 : (b + 1) * 16, :], tail], axis=1).astype(BF16)
            for j in range(nblk):
                h, i = j // (nblk // 2), j % (nblk // 2)
                b = me ^ sum((j >> dst & 1) << src for src, dst in gbits)
                gs_refs[h][i] = small[b]


def swap(x, hop, sizes):
    axis, mask = hop
    return lax.ppermute(x, axis, [(i, i ^ mask) for i in range(sizes[axis])])


def widen(x, order, sizes):
    for hop in order[:-1]:
        x = jnp.concatenate([x, swap(x, hop, sizes)], axis=0)
    return x, swap(x, order[-1], sizes)


def after(x, *deps):
    return lax.optimization_barrier((x,) + deps)[0]


def narrow_step(pair, hop, sizes):
    low, high = pair
    got = swap(high, hop, sizes)
    h = low.shape[0] // 2

    def add(sl):
        return low[sl].astype(F32) + got[sl].astype(F32)

    if h == 0:
        return add(slice(None))
    return add(slice(0, h)).astype(BF16), add(slice(h, 2 * h)).astype(BF16)


def whole(shape):
    zeros = (0,) * len(shape)
    return pl.BlockSpec(shape, lambda i: zeros, pipeline_mode=pl.Buffered(1))


def layer_calls(
    sc, tok, cot, idx, seg, kv_all, can, vec, bup, u_own, u_got, d_own, d_got,
    bits_u, bits_d, gbits_u, gbits_d, nblk, nseq, parts, moved=lambda dkv: None,
):
    d, ff, local = tok.shape[1], bup.shape[1], idx.shape[2]
    flat = tok.shape
    tile = R * local
    smem = pl.BlockSpec(memory_space=pltpu.SMEM)
    anywhere = pl.BlockSpec(memory_space=pl.ANY)
    params = pltpu.CompilerParams(vmem_limit_bytes=VMEM_LIMIT)
    shape = jax.ShapeDtypeStruct
    acc_shapes = (
        shape((d, ff), F32),
        shape((d, ff), F32),
        shape((d, d), F32),
        shape((d, d), F32),
    )
    vacc_shape = shape((104, d), F32)
    row0 = 0
    acc = None
    out = part = vacc = None
    for p, count in enumerate(parts):
        first, last = p == 0, p == len(parts) - 1
        steps = count // R
        base = row0 // R
        rowspec = pl.BlockSpec((tile, d), lambda i, base=base: (base + i, 0))
        kvspec = pl.BlockSpec((R, local, 128), lambda i: (i, 0, 0))
        ins = [sc, tok, cot, idx, seg] + kv_all[p] + [can, vec, bup, u_own, u_got, d_own, d_got]
        specs = [
            smem,
            rowspec,
            rowspec,
            pl.BlockSpec((R, 2, local), lambda i, base=base: (base + i, 0, 0)),
            pl.BlockSpec((R, 1, local * nseq), lambda i, base=base: (base + i, 0, 0)),
        ]
        specs += [kvspec] * nseq
        specs += [whole(can.shape), whole(vec.shape), whole(bup.shape)] + [anywhere] * 4
        alias = {}
        if not first:
            ins += list(acc) + [vacc, out, part]
            specs += [anywhere] * 7
            alias = {len(ins) - 2: 0, len(ins) - 1: 1}
        outs = [shape(flat, BF16), shape(flat, F32)]
        outs += [shape((count, local, 128), BF16)] * nseq + [vacc_shape]
        ospecs = [rowspec, rowspec] + [kvspec] * nseq + [whole(vacc_shape.shape)]
        scratch = []
        if last:
            sh_u, sh_d = (nblk // 2, 16, ff + d), (nblk // 2, 80, d)
            outs += [shape(sh_u, BF16)] * 2 + [shape(sh_d, BF16)] * 2
            ospecs += [whole(sh_u)] * 2 + [whole(sh_d)] * 2
            scratch += [pltpu.VMEM(a.shape, F32) for a in acc_shapes]
        else:
            outs += list(acc_shapes)
            ospecs += [whole(a.shape) for a in acc_shapes]
        wide = (tile, d)
        scratch += [
            pltpu.VMEM((d, ff), BF16),
            pltpu.VMEM((ff, d), BF16),
            pltpu.VMEM((d, d), BF16),
            pltpu.VMEM(wide, BF16),
            pltpu.VMEM(wide, F32),
            pltpu.VMEM((R, 2 * local, 128), BF16),
            pltpu.VMEM((R, 2 * local, 128), BF16),
            pltpu.VMEM((2, tile, 128), jnp.int32),
            pltpu.VMEM((2, tile, 128), F32),
            pltpu.VMEM((2, tile, 128), F32),
            pltpu.VMEM((2 * tile, 128), F32),
            pltpu.VMEM((R, 2 * local, nseq * local), BF16),
            pltpu.VMEM((2 * local, nseq * local), F32),
            pltpu.VMEM(wide, F32),
            pltpu.VMEM(wide, F32),
            pltpu.VMEM(wide, F32),
            pltpu.VMEM(wide, F32),
            pltpu.VMEM((tile, 128), F32),
            pltpu.VMEM(wide, BF16),
            pltpu.VMEM(wide, BF16),
            pltpu.VMEM((2, tile, 512), F32),
            pltpu.VMEM((2, tile, 512), F32),
            pltpu.VMEM((2, tile, 512), BF16),
            pltpu.VMEM((2, tile, 512), BF16),
            pltpu.VMEM((tile, 128), F32),
            pltpu.VMEM((tile, 128), BF16),
            pltpu.VMEM((d, tile), BF16),
            pltpu.VMEM((d, tile), BF16),
            pltpu.SemaphoreType.DMA((3,)),
            pltpu.SemaphoreType.DMA((6,)),
        ]
        cfg = (
            first,
            last,
            steps,
            bits_u,
            bits_d,
            gbits_u,
            gbits_d,
            nblk,
            nseq,
        )
        got = pl.pallas_call(
            functools.partial(kernel_b, cfg),
            grid=(steps,),
            out_shape=tuple(outs),
            in_specs=specs,
            out_specs=tuple(ospecs),
            scratch_shapes=scratch,
            input_output_aliases=alias,
            compiler_params=params,
            name="layer",
        )(*ins)
        out, part = got[0], got[1]
        dkv = got[2 : 2 + nseq]
        moved(dkv)
        vacc = got[2 + nseq]
        acc = got[3 + nseq :]
        row0 += count

    return out, part, vacc, acc


def body(
    sizes,
    tokens,
    cotangent,
    expert_index,
    segments,
    ln1_gain,
    ln1_bias,
    w_router,
    w_query,
    b_query,
    w_keyval,
    w_out,
    b_out,
    ln2_gain,
    ln2_bias,
    w_up,
    b_up,
    w_down,
    b_down,
):
    nseq, nbatch = sizes["seq"], sizes["batch"]
    rows_dev, local, d = tokens.shape
    ff = w_up.shape[1]
    experts = w_router.shape[1]
    group = max(1, 16 // w_query.shape[0])
    high = nbatch // group
    nblk = nseq * high
    bidx = lax.axis_index("batch")
    sidx = lax.axis_index("seq")
    blk = sidx * high + bidx // group
    sc = jnp.stack([blk, sidx]).astype(jnp.int32)

    groups = [[g * group + i for i in range(group)] for g in range(high)]

    def near(w):
        if group == 1:
            return w
        return lax.all_gather(w, "batch", axis=0, tiled=True, axis_index_groups=groups)

    def near_sum(g):
        if group == 1:
            return g
        return lax.psum_scatter(
            g, "batch", scatter_dimension=0, tiled=True, axis_index_groups=groups
        )

    bb = [("batch", group << i) for i in range((high - 1).bit_length())]
    zz = [("seq", 1 << i) for i in range((nseq - 1).bit_length())]
    core, xy = bb[0], bb[1:]

    def bit_of(hop):
        axis, mask = hop
        step = mask // group if axis == "batch" else mask * high
        return step.bit_length() - 1

    def gather_bits(order):
        return tuple((bit_of(hop), i) for i, hop in enumerate(order))

    def scatter_bits(order):
        return tuple((bit_of(hop), len(order) - 1 - i) for i, hop in enumerate(order))

    def weave(a, b):
        out = []
        for i in range(max(len(a), len(b))):
            out += list(a[i : i + 1]) + list(b[i : i + 1])
        return out

    order_a = zz[::-1] + xy + [core]
    order_u = zz[::-1] + xy + [core]
    order_d = zz[::-1] + xy[::-1] + [core]
    back_u = [core] + xy[::-1] + zz
    back_d = [core] + xy + zz
    back_s = [core] + xy[::-1] + zz

    def grow(x, hop):
        return jnp.concatenate([x, swap(x, hop, sizes)], axis=0)

    table = jnp.concatenate(
        [
            near(v)[None]
            for v in (ln1_gain, ln1_bias, b_query, b_out, ln2_gain, ln2_bias, b_down, b_down)
        ]
        + [jnp.transpose(near(w_router))],
        axis=0,
    )
    tail = lax.pad(near(b_up)[None], jnp.zeros((), BF16), ((0, 15, 0), (0, 48, 0)))
    pack = jnp.concatenate([near(w_query), near(w_keyval), table, tail], axis=1)[None]
    u = near(w_up)[None]
    dn = jnp.concatenate([near(w_down), near(w_out)], axis=0)[None]
    nz = len(zz)
    for n in range(nz):
        pack = grow(pack, order_a[n])
        u = grow(u, order_u[n])
        dn = grow(dn, order_d[n])
    for hop in order_a[nz:-1]:
        pack = grow(pack, hop)
    u = after(u, pack)
    dn = after(dn, pack)
    u = grow(u, order_u[nz])
    dn = grow(dn, order_d[nz])
    packs = [pack, swap(pack, core, sizes)]

    smem = pl.BlockSpec(memory_space=pltpu.SMEM)
    anywhere = pl.BlockSpec(memory_space=pl.ANY)
    params = pltpu.CompilerParams(vmem_limit_bytes=VMEM_LIMIT)
    shape = jax.ShapeDtypeStruct

    can, vec, bup, *kv_parts = pl.pallas_call(
        functools.partial(kernel_a, gather_bits(order_a), nblk, PARTS),
        out_shape=(
            shape((d, 768), BF16),
            shape((16, d), F32),
            shape((8, ff), F32),
        )
        + tuple(shape((n, local, 128), BF16) for n in PARTS),
        in_specs=[smem] + [pl.BlockSpec(memory_space=pltpu.VMEM)] * 3,
        out_specs=tuple(pl.BlockSpec(memory_space=pltpu.VMEM) for unused in range(3 + len(PARTS))),
        scratch_shapes=[pltpu.VMEM((nblk, 16, 768), BF16)],
        compiler_params=params,
        name="project",
    )(sc, *packs, tokens)

    flat = (rows_dev * local, d)
    tok = tokens.reshape(flat)
    cot = cotangent.reshape(flat)
    idx = jnp.transpose(expert_index, (0, 2, 1))
    seg = segments[:, None, :]
    tile = R * local

    kv_all = []

    def gather_kv(kv):
        kv_all.append([kv] + [swap(kv, ("seq", m), sizes) for m in range(1, nseq)])

    gather_kv(kv_parts[0])
    u = after(u, can)
    dn = after(dn, can)
    for n in range(nz + 1, len(order_u) - 1):
        u = grow(u, order_u[n])
        dn = grow(dn, order_d[n])
    u = after(u, *kv_all[0])
    dn = after(dn, *kv_all[0])
    us = [u, swap(u, core, sizes)]
    ds = [dn, swap(dn, core, sizes)]
    for kv in kv_parts[1:]:
        gather_kv(after(kv, *kv_all[-1]))
    dkv_all = []

    def moved(dkv):
        dkv_all.append([dkv[0]] + [swap(dkv[m], ("seq", m), sizes) for m in range(1, nseq)])

    out, part, vacc, acc = layer_calls(
        sc, tok, cot, idx, seg, kv_all, can, vec, bup, *us, *ds,
        gather_bits(order_u), gather_bits(order_d), scatter_bits(back_u), scatter_bits(back_d),
        nblk, nseq, PARTS, moved,
    )
    gu, gd = acc[0:2], acc[2:4]
    for n in range(len(PARTS) - 1):
        dkv_all[n] = [sum(v.astype(F32) for v in dkv_all[n]).astype(BF16)]
        gu, gd, dkv_all[n] = lax.optimization_barrier((gu, gd, dkv_all[n]))
    gu = narrow_step(gu, back_u[0], sizes)
    gd = narrow_step(gd, back_d[0], sizes)

    row0 = 0
    grad = None
    eacc = None
    for p, count in enumerate(PARTS):
        first, last = p == 0, p == len(PARTS) - 1
        steps = count // R
        base = row0 // R
        rowspec = pl.BlockSpec((tile, d), lambda i, base=base: (base + i, 0))
        kvspec = pl.BlockSpec((R, local, 128), lambda i: (i, 0, 0))
        if last:
            gu = narrow_step(gu, back_u[1], sizes)
            gd = narrow_step(gd, back_d[1], sizes)
        part = after(part, gu, gd)
        ins = [sc, part, tok] + list(dkv_all[p]) + [can, vec, vacc]
        specs = [smem, rowspec, rowspec] + [kvspec] * len(dkv_all[p])
        specs += [whole(can.shape), whole(vec.shape), whole(vacc.shape)]
        alias = {}
        if not first:
            ins += list(eacc) + [grad]
            specs += [whole((d, 128)), whole((16, d)), anywhere]
            alias = {len(ins) - 1: 0}
        outs = [shape(flat, BF16)]
        ospecs = [rowspec]
        scratch = []
        if last:
            outs += [shape((nblk // 2, 16, 256), BF16)] * 2
            ospecs += [whole((nblk // 2, 16, 256))] * 2
            scratch += [pltpu.VMEM((d, 128), F32), pltpu.VMEM((16, d), F32)]
        else:
            outs += [shape((d, 128), F32), shape((16, d), F32)]
            ospecs += [whole((d, 128)), whole((16, d))]
        scratch += [
            pltpu.VMEM((tile, d), F32),
            pltpu.VMEM((tile, d), BF16),
            pltpu.VMEM((tile, 128), BF16),
            pltpu.VMEM((nblk, 16, 256), BF16),
        ]
        cfg = (first, last, steps, scatter_bits(back_s), nblk, len(dkv_all[p]))
        got = pl.pallas_call(
            functools.partial(kernel_e, cfg),
            grid=(steps,),
            out_shape=tuple(outs),
            in_specs=specs,
            out_specs=tuple(ospecs),
            scratch_shapes=scratch,
            input_output_aliases=alias,
            compiler_params=params,
            name="finish",
        )(*ins)
        grad = got[0]
        eacc = got[1:]
        row0 += count
    gs = eacc
    for n in range(len(back_s)):
        gs = narrow_step(gs, back_s[n], sizes)
        if n + 2 < len(back_u):
            gu = narrow_step(gu, back_u[n + 2], sizes)
            gd = narrow_step(gd, back_d[n + 2], sizes)
        gs, gu, gd = lax.optimization_barrier((gs, gu, gd))
    gs, gu, gd = gs[0], gu[0], gd[0]

    def vector(v):
        return near_sum(gs[v, 128:144])

    return (
        out.reshape(tokens.shape),
        grad.reshape(tokens.shape),
        vector(0),
        vector(1),
        near_sum(jnp.transpose(gs[8 : 8 + experts, 128:144])),
        near_sum(gu[:, ff:]),
        vector(2),
        near_sum(gs[:, :128]),
        near_sum(gd[64:80]),
        vector(3),
        vector(4),
        vector(5),
        near_sum(gu[:, :ff]),
        near_sum(gs[0, 144:208]),
        near_sum(gd[:64]),
        vector(6),
    )


def solution(mesh):
    sizes = {name: mesh.shape[name] for name in ("seq", "batch")}
    both = ("seq", "batch")
    row = P("batch", "seq", None)
    vector, matrix = P(both), P(both, None)
    in_specs = (
        row,
        row,
        row,
        P("batch", None),
        vector,
        vector,
        matrix,
        matrix,
        vector,
        matrix,
        matrix,
        vector,
        vector,
        vector,
        matrix,
        vector,
        matrix,
        vector,
    )
    out_specs = (
        row,
        row,
        vector,
        vector,
        matrix,
        matrix,
        vector,
        matrix,
        matrix,
        vector,
        vector,
        vector,
        matrix,
        vector,
        matrix,
        vector,
    )
    return jax.shard_map(
        functools.partial(body, sizes),
        mesh=mesh,
        in_specs=in_specs,
        out_specs=out_specs,
        check_vma=False,
    )
```

```python
import functools

import jax
import jax.numpy as jnp
from jax import lax
from jax.experimental import pallas as pl
from jax.experimental.pallas import tpu as pltpu
from jax.sharding import PartitionSpec as P

EPS = 1e-05
NEG = -1e30
C0 = 0.7978845608028654
C1 = 0.7978845608028654 * 0.044715
PARTS = (4, 4)
LAG = 2
GSW = 1
R = 2
FC = 32
FU = 4
RU = 2
CH = 32
UN = 16
SC = 64
SU = 4
SD = 64
SV = 8
VMEM_LIMIT = 52 * 1024 * 1024
SMALL_LIMIT = 24 * 1024 * 1024
F32 = jnp.float32
BF16 = jnp.bfloat16


def mm(a, b):
    return lax.dot_general(a, b, (((1,), (0,)), ((), ())), preferred_element_type=F32)


def mmt(a, b):
    return lax.dot_general(a, b, (((1,), (1,)), ((), ())), preferred_element_type=F32)


def fold8(v):
    return jnp.sum(v.reshape(v.shape[0] // 8, 8, v.shape[1]), axis=0)


def norm_parts(x):
    mean = jnp.mean(x, axis=-1, keepdims=True)
    xc = x - mean
    rstd = lax.rsqrt(jnp.mean(xc * xc, axis=-1, keepdims=True) + EPS)
    return xc * rstd, rstd


def norm_back(d, xhat, rstd):
    return rstd * (
        d
        - jnp.mean(d, axis=-1, keepdims=True)
        - xhat * jnp.mean(d * xhat, axis=-1, keepdims=True)
    )


def rel(bits, v):
    j = 0
    for src, dst in bits:
        j = j | (((v >> src) & 1) << dst)
    return j


def kernel_a(bits, nblk, parts, sc, own, got, tok, can, vec, bup, *kvs):
    *kvs, pack = kvs
    me = sc[0]
    pack[0 : nblk // 2] = own[...]
    pack[nblk // 2 :] = got[...]
    lane = lax.broadcasted_iota(jnp.int32, (16, 128), 1)
    for g in range(nblk // 8):
        rows = jnp.zeros((16, 128), F32)
        for i in range(8):
            b = g * 8 + i
            block = pack[rel(bits, me ^ b)]
            can[b * 16 : (b + 1) * 16, 0:640] = block[:, 0:640]
            tail = block[:, 640:768].astype(F32)
            rows = jnp.where(lane >> 4 == i, pltpu.roll(tail, i * 16, 1) if i else tail, rows)
            line = pltpu.roll(tail, 112 if i % 2 == 0 else 48, 1)
            wide = line if i % 2 == 0 else jnp.where(lane >= 64, line, wide)
            if i % 2:
                bup[:, (b // 2) * 128 : (b // 2 + 1) * 128] = wide[0:8]
        vec[:, g * 128 : (g + 1) * 128] = rows
    router = jnp.concatenate([vec[8:16, :], jnp.zeros((120, vec.shape[1]), F32)], axis=0)
    can[:, 640:768] = jnp.transpose(router).astype(BF16)
    gain = vec[0:1, :]
    shift = vec[1:2, :]
    row = 0
    for kv, count in zip(kvs, parts):
        for r in range(count):
            xhat, unused = norm_parts(tok[row].astype(F32))
            normed = (xhat * gain + shift).astype(BF16)
            kv[r] = mm(normed, can[:, 512:640]).astype(BF16)
            row += 1


def kernel_b(cfg, *refs):
    first, last, steps, bits_u, bits_d, gbits_u, gbits_d, nblk, nseq = cfg
    refs = list(refs)

    def take(n):
        got = refs[:n]
        del refs[:n]
        return got

    sc, tok, cot, idx, seg = take(5)
    kvs = take(nseq)
    can, vec, bup = take(3)
    u_own, u_got, d_own, d_got = take(4)
    acc_in = []
    if not first:
        acc_in = take(5)
        take(2)
    out_ref, part_ref = take(2)
    dkvs = take(nseq)
    (vacc,) = take(1)
    if last:
        gu_refs = take(2)
        gd_refs = take(2)
    acc_up, acc_dn, acc_wo, acc_wq = take(4)
    (
        wup,
        wdn,
        wo,
        xn,
        q_s,
        qp,
        dp,
        idx_b,
        gate_b,
        cd,
        inner,
        prob,
        score,
        wide1,
        wide2,
        mid,
        xh2,
        rs2,
        n2,
        mix,
        hid,
        gac,
        act,
        ghd,
        low1,
        gl,
        n2_t,
        cot_t,
        wsem,
        asem,
    ) = refs

    me = sc[0]
    place = sc[1]
    step = pl.program_id(0)
    tile = tok.shape[0]
    local = tile // R
    ch = CH
    nch = tile // ch
    lane128 = lax.broadcasted_iota(jnp.int32, (ch, 128), 1)
    upper = lane128 >= 64
    half = lane128 >> 6
    accs = (acc_up, acc_dn, acc_wo, acc_wq, vacc)

    @pl.when(step == 0)
    def _():
        for piece, base in ((u_own, 0), (u_got, u_own.shape[0])):
            for c in range(piece.shape[0]):
                blk = me ^ sum(((base + c) >> dst & 1) << src for src, dst in bits_u)
                pltpu.make_async_copy(
                    piece.at[c], wup.at[pl.ds(pl.multiple_of(blk * 16, 16), 16), :], wsem.at[0]
                ).start()
        for piece, base in ((d_own, 0), (d_got, d_own.shape[0])):
            for c in range(piece.shape[0]):
                blk = me ^ sum(((base + c) >> dst & 1) << src for src, dst in bits_d)
                pltpu.make_async_copy(
                    piece.at[c, pl.ds(0, 64), :],
                    wdn.at[pl.ds(pl.multiple_of(blk * 64, 64), 64), :],
                    wsem.at[1],
                ).start()
                pltpu.make_async_copy(
                    piece.at[c, pl.ds(64, 16), :],
                    wo.at[pl.ds(pl.multiple_of(blk * 16, 16), 16), :],
                    wsem.at[2],
                ).start()
        if first:
            for a in accs:
                a[...] = jnp.zeros_like(a)
        else:
            for n, a in enumerate(accs):
                pltpu.make_async_copy(acc_in[n], a, asem.at[n]).start()

    gain1 = vec[0:1, :]
    shift1 = vec[1:2, :]
    bias_q = vec[2:3, :]
    bias_o = vec[3:4, :]
    gain2 = vec[4:5, :]
    shift2 = vec[5:6, :]
    bias_d = vec[6:7, :]

    def norm_chunk(c, carry):
        sl = pl.ds(pl.multiple_of(c * ch, ch), ch)
        xhat, unused = norm_parts(tok[sl, :].astype(F32))
        xn[sl, :] = (xhat * gain1 + shift1).astype(BF16)
        return carry

    lax.fori_loop(0, nch, norm_chunk, 0, unroll=UN)
    q_s[...] = mm(xn[...], can[:, 0:512])
    low1[...] = mm(xn[...], can[:, 640:768])
    for r in range(R):
        for s in range(2):
            line = idx[r, s : s + 1, :].astype(F32)
            idx_b[s, r * local : (r + 1) * local, :] = jnp.transpose(
                jnp.broadcast_to(line, (128, local))
            ).astype(jnp.int32)

    def gate_chunk(c, carry):
        sl = pl.ds(pl.multiple_of(c * ch, ch), ch)
        logits = low1[sl, :]
        i0 = idx_b[0, sl, :]
        i1 = idx_b[1, sl, :]
        top = jnp.max(jnp.where(lane128 < 8, logits, -jnp.inf), axis=-1, keepdims=True)
        e0 = jnp.exp(jnp.sum(jnp.where(lane128 == i0, logits, 0.0), axis=-1, keepdims=True) - top)
        e1 = jnp.exp(jnp.sum(jnp.where(lane128 == i1, logits, 0.0), axis=-1, keepdims=True) - top)
        total = e0 + e1
        gate_b[0, sl, :] = jnp.broadcast_to(e0 / total, (ch, 128))
        gate_b[1, sl, :] = jnp.broadcast_to(e1 / total, (ch, 128))
        r = c // (local // ch)
        at = pl.multiple_of((c % (local // ch)) * ch, ch)
        f0 = jnp.zeros((ch, 128), F32)
        f1 = jnp.zeros((ch, 128), F32)
        for b in range(4):
            q = (q_s[sl, b * 128 : (b + 1) * 128] + bias_q[:, b * 128 : (b + 1) * 128]) * 0.125
            f0 = f0 + jnp.where(half + 2 * b == i0, q, 0.0)
            f1 = f1 + jnp.where(half + 2 * b == i1, q, 0.0)
        f0 = f0 + pltpu.roll(f0, 64, 1)
        f1 = f1 + pltpu.roll(f1, 64, 1)
        qp[r, pl.ds(at, ch), :] = jnp.where(upper, 0.0, f0).astype(BF16)
        qp[r, pl.ds(local + at, ch), :] = jnp.where(upper, 0.0, f1).astype(BF16)
        return carry

    lax.fori_loop(0, nch, gate_chunk, 0, unroll=UN)

    def attend(r, outer):
        for m in range(nseq):
            score[r, :, m * local : (m + 1) * local] = mmt(qp[r], kvs[m][r])
        seg_k = jnp.concatenate(
            [
                seg[r, :, pl.ds(pl.multiple_of((place ^ m) * local, 128), local)]
                for m in range(nseq)
            ],
            axis=1,
        )
        own = seg[r, :, pl.ds(pl.multiple_of(place * local, 128), local)].astype(F32)
        inner[pl.ds(pl.multiple_of(r * local, local), local), :] = jnp.transpose(
            jnp.broadcast_to(own, (128, local))
        )

        def soft_chunk(c, carry):
            at = pl.multiple_of(c * SC, SC)
            mine = pl.ds(pl.multiple_of(r * local + at, SC), SC)
            match = inner[mine, 0:1].astype(jnp.int32) == seg_k
            for s in range(2):
                sl = pl.ds(pl.multiple_of(s * local + at, SC), SC)
                sc_ = jnp.where(match, score[r, sl, :], NEG)
                num = jnp.exp(sc_ - jnp.max(sc_, axis=-1, keepdims=True))
                total = jnp.sum(num, axis=-1, keepdims=True)
                prob[r, sl, :] = (num * (1.0 / total)).astype(BF16)
            return carry

        lax.fori_loop(0, local // SC, soft_chunk, 0, unroll=SU)
        ctx = jnp.zeros((2 * local, 128), F32)
        for m in range(nseq):
            ctx = ctx + mm(prob[r, :, m * local : (m + 1) * local], kvs[m][r])
        up2 = lax.broadcasted_iota(jnp.int32, ctx.shape, 1) >= 64
        ctx = jnp.where(up2, ctx, 0.0)
        ctx = ctx + pltpu.roll(ctx, 64, 1)
        own_rows = pl.ds(pl.multiple_of(r * local, local), local)
        cd[0, own_rows, :] = ctx[:local]
        cd[1, own_rows, :] = ctx[local:]
        return outer

    for r in range(R):
        attend(r, 0)

    @pl.when(step == 0)
    def _():
        for n, w in enumerate((wup, wdn, wo)):
            pltpu.make_async_copy(w, w, wsem.at[n]).wait()
        if not first:
            for n, a in enumerate(accs):
                pltpu.make_async_copy(acc_in[n], a, asem.at[n]).wait()

    def mix_chunk(c, carry):
        sl = pl.ds(pl.multiple_of(c * ch, ch), ch)
        i0 = idx_b[0, sl, :]
        i1 = idx_b[1, sl, :]
        m0 = gate_b[0, sl, :] * cd[0, sl, :]
        m1 = gate_b[1, sl, :] * cd[1, sl, :]
        for b in range(4):
            mix[sl, b * 128 : (b + 1) * 128] = jnp.where(
                half + 2 * b == i0, m0, jnp.where(half + 2 * b == i1, m1, 0.0)
            ).astype(BF16)
        return carry

    lax.fori_loop(0, nch, mix_chunk, 0, unroll=UN)
    wide1[...] = mm(mix[...], wo[...])

    def mid_chunk(c, carry):
        sl = pl.ds(pl.multiple_of(c * ch, ch), ch)
        middle = tok[sl, :].astype(F32) + (wide1[sl, :] + bias_o)
        mid[sl, :] = middle
        xhat, rstd = norm_parts(middle)
        xh2[sl, :] = xhat
        rs2[sl, :] = jnp.broadcast_to(rstd, (ch, 128))
        n2[sl, :] = (xhat * gain2 + shift2).astype(BF16)
        return carry

    lax.fori_loop(0, nch, mid_chunk, 0, unroll=UN)

    n2_t[...] = jnp.transpose(n2[...])
    cot_t[...] = jnp.transpose(cot[...])
    width = hid.shape[2]
    wide1[...] = jnp.zeros_like(wide1)
    wide2[...] = jnp.zeros_like(wide2)

    def hidden_block(j, carry):
        js = slice(j * width, (j + 1) * width)
        k = j % 2
        hid[k] = mm(n2[...], wup[:, js])
        gac[k] = mmt(cot[...], wdn[js, :])
        bias = bup[0:1, js]
        total = jnp.zeros((8, width), F32)
        for c in range(tile // FC):
            sl = slice(c * FC, (c + 1) * FC)
            h = hid[k, sl, :] + bias
            h2 = h * h
            t = jnp.tanh(h * (C0 + C1 * h2))
            hh = 0.5 * h
            act[k, sl, :] = (hh + hh * t).astype(BF16)
            slope = (0.5 + 0.5 * t) + hh * (1.0 - t * t) * (C0 + (3.0 * C1) * h2)
            g = (gac[k, sl, :] * slope).astype(BF16)
            ghd[k, sl, :] = g
            total = total + fold8(g.astype(F32))
        vacc[(7 + j) * 8 : (8 + j) * 8, :] += total
        wide1[...] += mm(act[k], wdn[js, :])
        wide2[...] += mmt(ghd[k], wup[:, js])
        acc_up[:, js] += mm(n2_t[...], ghd[k])
        acc_dn[:, js] += mm(cot_t[...], act[k])
        return carry

    for j in range(wup.shape[1] // width):
        hidden_block(j, 0)

    def out_chunk(c, carry):
        sl = pl.ds(pl.multiple_of(c * ch, ch), ch)
        out_ref[sl, :] = (mid[sl, :] + (wide1[sl, :] + bias_d)).astype(BF16)
        ct = cot[sl, :].astype(F32)
        g = wide2[sl, :]
        xhat = xh2[sl, :]
        gm = ct + norm_back(g * gain2, xhat, rs2[sl, 0:1])
        mid[sl, :] = gm
        low = gm.astype(BF16)
        n2[sl, :] = low
        vacc[24:32, :] += fold8(low.astype(F32))
        vacc[32:40, :] += fold8(g * xhat)
        vacc[40:48, :] += fold8(g)
        vacc[48:56, :] += fold8(ct)
        return carry

    lax.fori_loop(0, nch, out_chunk, 0, unroll=UN)

    acc_wo[...] += mm(jnp.transpose(mix[...]), n2[...])
    wide1[...] = mmt(n2[...], wo[...])

    def gate_back_chunk(c, carry):
        sl = pl.ds(pl.multiple_of(c * ch, ch), ch)
        i0 = idx_b[0, sl, :]
        i1 = idx_b[1, sl, :]
        f0 = jnp.zeros((ch, 128), F32)
        f1 = jnp.zeros((ch, 128), F32)
        for b in range(4):
            g = wide1[sl, b * 128 : (b + 1) * 128]
            f0 = f0 + jnp.where(half + 2 * b == i0, g, 0.0)
            f1 = f1 + jnp.where(half + 2 * b == i1, g, 0.0)
        f0 = jnp.where(upper, f0 + pltpu.roll(f0, 64, 1), 0.0)
        f1 = jnp.where(upper, f1 + pltpu.roll(f1, 64, 1), 0.0)
        c0 = cd[0, sl, :]
        c1 = cd[1, sl, :]
        g0 = gate_b[0, sl, :]
        g1 = gate_b[1, sl, :]
        gg0 = jnp.sum(f0 * c0, axis=-1, keepdims=True)
        gg1 = jnp.sum(f1 * c1, axis=-1, keepdims=True)
        both = g0 * gg0 + g1 * gg1
        gl[sl, :] = jnp.where(
            lane128 == i0, g0 * (gg0 - both), jnp.where(lane128 == i1, g1 * (gg1 - both), 0.0)
        ).astype(BF16)
        d0 = (g0 * f0).astype(BF16)
        d1 = (g1 * f1).astype(BF16)
        r = c // (local // ch)
        at = pl.multiple_of((c % (local // ch)) * ch, ch)
        s0 = pl.ds(r * 2 * local + at, ch)
        s1 = pl.ds(r * 2 * local + local + at, ch)
        dp[r, pl.ds(at, ch), :] = d0
        dp[r, pl.ds(local + at, ch), :] = d1
        inner[s0, :] = jnp.broadcast_to(
            jnp.sum(d0.astype(F32) * c0, axis=-1, keepdims=True), (ch, 128)
        )
        inner[s1, :] = jnp.broadcast_to(
            jnp.sum(d1.astype(F32) * c1, axis=-1, keepdims=True), (ch, 128)
        )
        return carry

    lax.fori_loop(0, nch, gate_back_chunk, 0, unroll=UN)

    width = hid.shape[2]

    def attend_back(r, outer):
        for m in range(nseq):
            score[r, :, m * local : (m + 1) * local] = mmt(dp[r], kvs[m][r])
        dsc = (act, ghd)[r % 2]

        def score_chunk(c, carry):
            at = pl.multiple_of(c * SD, SD)
            sl = pl.ds(at, SD)
            inn = inner[pl.ds(pl.multiple_of(r * 2 * local + at, SD), SD), 0:1]
            for k in range(2):
                ks = slice(k * width, (k + 1) * width)
                dsc[k, sl, :] = (prob[r, sl, ks].astype(F32) * (score[r, sl, ks] - inn)).astype(BF16)
            return carry

        lax.fori_loop(0, 2 * local // SD, score_chunk, 0, unroll=SV)
        q_t = jnp.transpose(qp[r])
        d_t = jnp.transpose(dp[r])
        dq = jnp.zeros((2 * local, 128), F32)
        for m in range(nseq):
            k = m * local // width
            ks = slice(m * local - k * width, m * local - k * width + local)
            ds_m = dsc[k, :, ks]
            dq = dq + mm(ds_m, kvs[m][r])
            dkv_t = mm(q_t, ds_m) + mm(d_t, prob[r, :, m * local : (m + 1) * local])
            dkvs[m][r] = jnp.transpose(dkv_t).astype(BF16)
        up2 = lax.broadcasted_iota(jnp.int32, dq.shape, 1) >= 64
        dq = jnp.where(up2, 0.0, dq) * 0.125
        dq = dq + pltpu.roll(dq, 64, 1)
        own_rows = pl.ds(pl.multiple_of(r * local, local), local)
        cd[0, own_rows, :] = dq[:local]
        cd[1, own_rows, :] = dq[local:]
        return outer

    for r in range(R):
        attend_back(r, 0)

    def query_chunk(c, carry):
        sl = pl.ds(pl.multiple_of(c * ch, ch), ch)
        i0 = idx_b[0, sl, :]
        i1 = idx_b[1, sl, :]
        m0 = cd[0, sl, :]
        m1 = cd[1, sl, :]
        for b in range(4):
            low = jnp.where(
                half + 2 * b == i0, m0, jnp.where(half + 2 * b == i1, m1, 0.0)
            ).astype(BF16)
            mix[sl, b * 128 : (b + 1) * 128] = low
            vacc[16:24, b * 128 : (b + 1) * 128] += fold8(low.astype(F32))
        return carry

    lax.fori_loop(0, nch, query_chunk, 0, unroll=UN)
    xn_t = jnp.transpose(xn[...])
    acc_wq[...] += mm(xn_t, mix[...])
    vacc[88:104, :] += mm(jnp.transpose(gl[...])[0:16], xn[...])
    wide1[...] = mmt(mix[...], can[:, 0:512]) + mmt(gl[...], can[:, 640:768])

    def part_chunk(c, carry):
        sl = pl.ds(pl.multiple_of(c * ch, ch), ch)
        xhat, rstd = norm_parts(tok[sl, :].astype(F32))
        g = wide1[sl, :]
        part_ref[sl, :] = mid[sl, :] + norm_back(g * gain1, xhat, rstd)
        vacc[0:8, :] += fold8(g * xhat)
        vacc[8:16, :] += fold8(g)
        return carry

    lax.fori_loop(0, nch, part_chunk, 0, unroll=UN)

    if last:

        @pl.when(step == steps - 1)
        def _():
            for c in range(wdn.shape[0] // 128):
                cs = slice(c * 128, (c + 1) * 128)
                wdn[cs, :] = jnp.transpose(acc_dn[:, cs].astype(BF16))
            for j in range(nblk):
                h, i = j // (nblk // 2), j % (nblk // 2)
                b = me ^ sum((j >> dst & 1) << src for src, dst in gbits_u)
                rows = pl.ds(pl.multiple_of(b * 16, 16), 16)
                gu_refs[h][i, :, 0:2048] = acc_up[rows, :].astype(BF16)
                gu_refs[h][i, :, 2048:2560] = acc_wq[rows, :].astype(BF16)
                b = me ^ sum((j >> dst & 1) << src for src, dst in gbits_d)
                gd_refs[h][i, 0:64, :] = wdn[pl.ds(pl.multiple_of(b * 64, 64), 64), :]
                rows = pl.ds(pl.multiple_of(b * 16, 16), 16)
                gd_refs[h][i, 64:80, :] = acc_wo[rows, :].astype(BF16)


def kernel_e(cfg, *refs):
    first, last, steps, gbits, nblk, nseq = cfg
    refs = list(refs)

    def take(n):
        got = refs[:n]
        del refs[:n]
        return got

    sc, part, tok = take(3)
    dkvs = take(nseq)
    can, vec, vacc = take(3)
    acc_in = []
    if not first:
        acc_in = take(2)
        take(1)
    (out_ref,) = take(1)
    if last:
        gs_refs = take(2)
    acc_kv, acc_l = take(2)
    wide, xn, dk, small = refs
    me = sc[0]
    step = pl.program_id(0)
    tile = tok.shape[0]
    local = tile // R
    ch = CH
    nch = tile // ch
    gain = vec[0:1, :]
    shift = vec[1:2, :]

    @pl.when(step == 0)
    def _():
        if first:
            acc_kv[...] = jnp.zeros_like(acc_kv)
            acc_l[...] = jnp.zeros_like(acc_l)
        else:
            acc_kv[...] = acc_in[0][...]
            acc_l[...] = acc_in[1][...]

    for r in range(R):
        total = dkvs[0][r].astype(F32)
        for m in range(1, nseq):
            total = total + dkvs[m][r].astype(F32)
        dk[r * local : (r + 1) * local, :] = total.astype(BF16)
    wide[...] = mmt(dk[...], can[:, 512:640])

    def chunk(c, carry):
        sl = pl.ds(pl.multiple_of(c * ch, ch), ch)
        xhat, rstd = norm_parts(tok[sl, :].astype(F32))
        xn[sl, :] = (xhat * gain + shift).astype(BF16)
        g = wide[sl, :]
        out_ref[sl, :] = (part[sl, :] + norm_back(g * gain, xhat, rstd)).astype(BF16)
        acc_l[0:8, :] += fold8(g * xhat)
        acc_l[8:16, :] += fold8(g)
        return carry

    lax.fori_loop(0, nch, chunk, 0, unroll=UN)
    acc_kv[...] += mm(jnp.transpose(xn[...]), dk[...])

    if last:

        @pl.when(step == steps - 1)
        def _():
            row = lax.broadcasted_iota(jnp.int32, (16, 512), 0)
            table = jnp.zeros((16, 512), F32)
            for v in range(7):
                line = vacc[v * 8 : (v + 1) * 8, :]
                if v < 2:
                    line = line + acc_l[v * 8 : (v + 1) * 8, :]
                table = jnp.where(row == v, jnp.sum(line, axis=0, keepdims=True), table)
            router = vacc[88:104, :][0:8]
            table = table + jnp.concatenate([jnp.zeros((8, 512), F32), router], axis=0)
            ups = [
                jnp.sum(vacc[(7 + b) * 8 : (8 + b) * 8, :], axis=0, keepdims=True)
                for b in range(4)
            ]
            lane = lax.broadcasted_iota(jnp.int32, (16, 128), 1)
            first_row = lax.broadcasted_iota(jnp.int32, (16, 128), 0) == 0
            for b in range(nblk):
                g, i = b // 8, b % 8
                rows = table[:, g * 128 : (g + 1) * 128]
                if i:
                    rows = pltpu.roll(rows, 128 - i * 16, 1)
                c = b * 64 // 512
                at = (b * 64 % 512) // 128 * 128
                line = jnp.broadcast_to(ups[c][:, at : at + 128], (16, 128))
                line = pltpu.roll(line, 16 if b % 2 == 0 else 80, 1)
                tail = jnp.where(
                    lane < 16, rows, jnp.where(first_row & (lane < 80), line, 0.0)
                )
                small[b] = jnp.concatenate([acc_kv[b * 16 : (b + 1) * 16, :], tail], axis=1).astype(BF16)
            for j in range(nblk):
                h, i = j // (nblk // 2), j % (nblk // 2)
                b = me ^ sum((j >> dst & 1) << src for src, dst in gbits)
                gs_refs[h][i] = small[b]


def swap(x, hop, sizes):
    axis, mask = hop
    return lax.ppermute(x, axis, [(i, i ^ mask) for i in range(sizes[axis])])


def widen(x, order, sizes):
    for hop in order[:-1]:
        x = jnp.concatenate([x, swap(x, hop, sizes)], axis=0)
    return x, swap(x, order[-1], sizes)


def after(x, *deps):
    return lax.optimization_barrier((x,) + deps)[0]


def narrow_step(pair, hop, sizes):
    low, high = pair
    got = swap(high, hop, sizes)
    h = low.shape[0] // 2

    def add(sl):
        return low[sl].astype(F32) + got[sl].astype(F32)

    if h == 0:
        return add(slice(None))
    return add(slice(0, h)).astype(BF16), add(slice(h, 2 * h)).astype(BF16)


def whole(shape):
    zeros = (0,) * len(shape)
    return pl.BlockSpec(shape, lambda i: zeros, pipeline_mode=pl.Buffered(1))


def layer_calls(
    sc, tok, cot, idx, seg, kv_all, can, vec, bup, u_own, u_got, d_own, d_got,
    bits_u, bits_d, gbits_u, gbits_d, nblk, nseq, parts, moved=lambda dkv: None,
):
    d, ff, local = tok.shape[1], bup.shape[1], idx.shape[2]
    flat = tok.shape
    tile = R * local
    smem = pl.BlockSpec(memory_space=pltpu.SMEM)
    anywhere = pl.BlockSpec(memory_space=pl.ANY)
    params = pltpu.CompilerParams(vmem_limit_bytes=VMEM_LIMIT)
    shape = jax.ShapeDtypeStruct
    acc_shapes = (
        shape((d, ff), F32),
        shape((d, ff), F32),
        shape((d, d), F32),
        shape((d, d), F32),
    )
    vacc_shape = shape((104, d), F32)
    row0 = 0
    acc = None
    out = part = vacc = None
    for p, count in enumerate(parts):
        first, last = p == 0, p == len(parts) - 1
        steps = count // R
        base = row0 // R
        rowspec = pl.BlockSpec((tile, d), lambda i, base=base: (base + i, 0))
        kvspec = pl.BlockSpec((R, local, 128), lambda i: (i, 0, 0))
        ins = [sc, tok, cot, idx, seg] + kv_all[p] + [can, vec, bup, u_own, u_got, d_own, d_got]
        specs = [
            smem,
            rowspec,
            rowspec,
            pl.BlockSpec((R, 2, local), lambda i, base=base: (base + i, 0, 0)),
            pl.BlockSpec((R, 1, local * nseq), lambda i, base=base: (base + i, 0, 0)),
        ]
        specs += [kvspec] * nseq
        specs += [whole(can.shape), whole(vec.shape), whole(bup.shape)] + [anywhere] * 4
        alias = {}
        if not first:
            ins += list(acc) + [vacc, out, part]
            specs += [anywhere] * 7
            alias = {len(ins) - 2: 0, len(ins) - 1: 1}
        outs = [shape(flat, BF16), shape(flat, F32)]
        outs += [shape((count, local, 128), BF16)] * nseq + [vacc_shape]
        ospecs = [rowspec, rowspec] + [kvspec] * nseq + [whole(vacc_shape.shape)]
        scratch = []
        if last:
            sh_u, sh_d = (nblk // 2, 16, ff + d), (nblk // 2, 80, d)
            outs += [shape(sh_u, BF16)] * 2 + [shape(sh_d, BF16)] * 2
            ospecs += [whole(sh_u)] * 2 + [whole(sh_d)] * 2
            scratch += [pltpu.VMEM(a.shape, F32) for a in acc_shapes]
        else:
            outs += list(acc_shapes)
            ospecs += [whole(a.shape) for a in acc_shapes]
        wide = (tile, d)
        scratch += [
            pltpu.VMEM((d, ff), BF16),
            pltpu.VMEM((ff, d), BF16),
            pltpu.VMEM((d, d), BF16),
            pltpu.VMEM(wide, BF16),
            pltpu.VMEM(wide, F32),
            pltpu.VMEM((R, 2 * local, 128), BF16),
            pltpu.VMEM((R, 2 * local, 128), BF16),
            pltpu.VMEM((2, tile, 128), jnp.int32),
            pltpu.VMEM((2, tile, 128), F32),
            pltpu.VMEM((2, tile, 128), F32),
            pltpu.VMEM((2 * tile, 128), F32),
            pltpu.VMEM((R, 2 * local, nseq * local), BF16),
            pltpu.VMEM((R, 2 * local, nseq * local), F32),
            pltpu.VMEM(wide, F32),
            pltpu.VMEM(wide, F32),
            pltpu.VMEM(wide, F32),
            pltpu.VMEM(wide, F32),
            pltpu.VMEM((tile, 128), F32),
            pltpu.VMEM(wide, BF16),
            pltpu.VMEM(wide, BF16),
            pltpu.VMEM((2, tile, 512), F32),
            pltpu.VMEM((2, tile, 512), F32),
            pltpu.VMEM((2, tile, 512), BF16),
            pltpu.VMEM((2, tile, 512), BF16),
            pltpu.VMEM((tile, 128), F32),
            pltpu.VMEM((tile, 128), BF16),
            pltpu.VMEM((d, tile), BF16),
            pltpu.VMEM((d, tile), BF16),
            pltpu.SemaphoreType.DMA((3,)),
            pltpu.SemaphoreType.DMA((6,)),
        ]
        cfg = (
            first,
            last,
            steps,
            bits_u,
            bits_d,
            gbits_u,
            gbits_d,
            nblk,
            nseq,
        )
        got = pl.pallas_call(
            functools.partial(kernel_b, cfg),
            grid=(steps,),
            out_shape=tuple(outs),
            in_specs=specs,
            out_specs=tuple(ospecs),
            scratch_shapes=scratch,
            input_output_aliases=alias,
            compiler_params=params,
            name="layer",
        )(*ins)
        out, part = got[0], got[1]
        dkv = got[2 : 2 + nseq]
        moved(dkv)
        vacc = got[2 + nseq]
        acc = got[3 + nseq :]
        row0 += count

    return out, part, vacc, acc


def body(
    sizes,
    tokens,
    cotangent,
    expert_index,
    segments,
    ln1_gain,
    ln1_bias,
    w_router,
    w_query,
    b_query,
    w_keyval,
    w_out,
    b_out,
    ln2_gain,
    ln2_bias,
    w_up,
    b_up,
    w_down,
    b_down,
):
    nseq, nbatch = sizes["seq"], sizes["batch"]
    rows_dev, local, d = tokens.shape
    ff = w_up.shape[1]
    experts = w_router.shape[1]
    group = max(1, 16 // w_query.shape[0])
    high = nbatch // group
    nblk = nseq * high
    bidx = lax.axis_index("batch")
    sidx = lax.axis_index("seq")
    blk = sidx * high + bidx // group
    sc = jnp.stack([blk, sidx]).astype(jnp.int32)

    groups = [[g * group + i for i in range(group)] for g in range(high)]

    def near(w):
        if group == 1:
            return w
        return lax.all_gather(w, "batch", axis=0, tiled=True, axis_index_groups=groups)

    def near_sum(g):
        if group == 1:
            return g
        return lax.psum_scatter(
            g, "batch", scatter_dimension=0, tiled=True, axis_index_groups=groups
        )

    bb = [("batch", group << i) for i in range((high - 1).bit_length())]
    zz = [("seq", 1 << i) for i in range((nseq - 1).bit_length())]
    core, xy = bb[0], bb[1:]

    def bit_of(hop):
        axis, mask = hop
        step = mask // group if axis == "batch" else mask * high
        return step.bit_length() - 1

    def gather_bits(order):
        return tuple((bit_of(hop), i) for i, hop in enumerate(order))

    def scatter_bits(order):
        return tuple((bit_of(hop), len(order) - 1 - i) for i, hop in enumerate(order))

    def weave(a, b):
        out = []
        for i in range(max(len(a), len(b))):
            out += list(a[i : i + 1]) + list(b[i : i + 1])
        return out

    order_a = zz[::-1] + xy + [core]
    order_u = zz[::-1] + xy + [core]
    order_d = zz[::-1] + xy[::-1] + [core]
    back_u = [core] + xy[::-1] + zz
    back_d = [core] + xy + zz
    if GSW == 1:
        back_u = [core] + xy[::-1][:1] + zz[:1] + xy[::-1][1:] + zz[1:]
    if GSW == 2:
        back_u = [core] + xy[::-1][:1] + zz[:1] + zz[1:] + xy[::-1][1:]
    back_s = [core] + xy[::-1] + zz

    def grow(x, hop):
        return jnp.concatenate([x, swap(x, hop, sizes)], axis=0)

    table = jnp.concatenate(
        [
            near(v)[None]
            for v in (ln1_gain, ln1_bias, b_query, b_out, ln2_gain, ln2_bias, b_down, b_down)
        ]
        + [jnp.transpose(near(w_router))],
        axis=0,
    )
    tail = lax.pad(near(b_up)[None], jnp.zeros((), BF16), ((0, 15, 0), (0, 48, 0)))
    pack = jnp.concatenate([near(w_query), near(w_keyval), table, tail], axis=1)[None]
    u = near(w_up)[None]
    dn = jnp.concatenate([near(w_down), near(w_out)], axis=0)[None]
    nz = len(zz)
    for n in range(nz):
        pack = grow(pack, order_a[n])
        u = grow(u, order_u[n])
        dn = grow(dn, order_d[n])
    for hop in order_a[nz:-1]:
        pack = grow(pack, hop)
    u = grow(after(u, pack), order_u[nz])
    dn = grow(after(dn, pack), order_d[nz])
    packs = [pack, swap(pack, core, sizes)]

    smem = pl.BlockSpec(memory_space=pltpu.SMEM)
    anywhere = pl.BlockSpec(memory_space=pl.ANY)
    params = pltpu.CompilerParams(vmem_limit_bytes=SMALL_LIMIT)
    shape = jax.ShapeDtypeStruct

    can, vec, bup, *kv_parts = pl.pallas_call(
        functools.partial(kernel_a, gather_bits(order_a), nblk, PARTS),
        out_shape=(
            shape((d, 768), BF16),
            shape((16, d), F32),
            shape((8, ff), F32),
        )
        + tuple(shape((n, local, 128), BF16) for n in PARTS),
        in_specs=[smem] + [pl.BlockSpec(memory_space=pltpu.VMEM)] * 3,
        out_specs=tuple(pl.BlockSpec(memory_space=pltpu.VMEM) for unused in range(3 + len(PARTS))),
        scratch_shapes=[pltpu.VMEM((nblk, 16, 768), BF16)],
        compiler_params=params,
        name="project",
    )(sc, *packs, tokens)

    flat = (rows_dev * local, d)
    tok = tokens.reshape(flat)
    cot = cotangent.reshape(flat)
    idx = jnp.transpose(expert_index, (0, 2, 1))
    seg = segments[:, None, :]
    tile = R * local

    kv_all = []

    def gather_kv(kv):
        kv_all.append([kv] + [swap(kv, ("seq", m), sizes) for m in range(1, nseq)])

    gather_kv(kv_parts[0])
    u = after(u, kv_all[0][1])
    dn = after(dn, kv_all[0][1])
    for n in range(nz + 1, len(order_u) - 1):
        u = grow(u, order_u[n])
        dn = grow(dn, order_d[n])
    u = after(u, *kv_all[0])
    dn = after(dn, *kv_all[0])
    us = [u, swap(u, core, sizes)]
    ds = [dn, swap(dn, core, sizes)]
    for kv in kv_parts[1:]:
        gather_kv(after(kv, *kv_all[-1]))
    dkv_all = []

    def moved(dkv):
        dkv_all.append([dkv[0]] + [swap(dkv[m], ("seq", m), sizes) for m in range(1, nseq)])

    out, part, vacc, acc = layer_calls(
        sc, tok, cot, idx, seg, kv_all, can, vec, bup, *us, *ds,
        gather_bits(order_u), gather_bits(order_d), scatter_bits(back_u), scatter_bits(back_d),
        nblk, nseq, PARTS, moved,
    )
    gu, gd = acc[0:2], acc[2:4]
    for n in range(len(PARTS) - 1):
        dkv_all[n] = [sum(v.astype(F32) for v in dkv_all[n]).astype(BF16)]
        gu, gd, dkv_all[n] = lax.optimization_barrier((gu, gd, dkv_all[n]))
    gu = narrow_step(gu, back_u[0], sizes)
    gd = narrow_step(gd, back_d[0], sizes)

    row0 = 0
    grad = None
    eacc = None
    for p, count in enumerate(PARTS):
        first, last = p == 0, p == len(PARTS) - 1
        steps = count // R
        base = row0 // R
        rowspec = pl.BlockSpec((tile, d), lambda i, base=base: (base + i, 0))
        kvspec = pl.BlockSpec((R, local, 128), lambda i: (i, 0, 0))
        if last:
            gu = narrow_step(gu, back_u[1], sizes)
            gd = narrow_step(gd, back_d[1], sizes)
        part = after(part, gu, gd)
        ins = [sc, part, tok] + list(dkv_all[p]) + [can, vec, vacc]
        specs = [smem, rowspec, rowspec] + [kvspec] * len(dkv_all[p])
        specs += [whole(can.shape), whole(vec.shape), whole(vacc.shape)]
        alias = {}
        if not first:
            ins += list(eacc) + [grad]
            specs += [whole((d, 128)), whole((16, d)), anywhere]
            alias = {len(ins) - 1: 0}
        outs = [shape(flat, BF16)]
        ospecs = [rowspec]
        scratch = []
        if last:
            outs += [shape((nblk // 2, 16, 256), BF16)] * 2
            ospecs += [whole((nblk // 2, 16, 256))] * 2
            scratch += [pltpu.VMEM((d, 128), F32), pltpu.VMEM((16, d), F32)]
        else:
            outs += [shape((d, 128), F32), shape((16, d), F32)]
            ospecs += [whole((d, 128)), whole((16, d))]
        scratch += [
            pltpu.VMEM((tile, d), F32),
            pltpu.VMEM((tile, d), BF16),
            pltpu.VMEM((tile, 128), BF16),
            pltpu.VMEM((nblk, 16, 256), BF16),
        ]
        cfg = (first, last, steps, scatter_bits(back_s), nblk, len(dkv_all[p]))
        got = pl.pallas_call(
            functools.partial(kernel_e, cfg),
            grid=(steps,),
            out_shape=tuple(outs),
            in_specs=specs,
            out_specs=tuple(ospecs),
            scratch_shapes=scratch,
            input_output_aliases=alias,
            compiler_params=params,
            name="finish",
        )(*ins)
        grad = got[0]
        eacc = got[1:]
        row0 += count
    gs = eacc
    gu, gd, unused = lax.optimization_barrier((gu, gd, dkv_all[-1]))
    later = [(gu, gd)]
    for n in range(2, len(back_u)):
        gu = narrow_step(gu, back_u[n], sizes)
        gd = narrow_step(gd, back_d[n], sizes)
        later.append((gu, gd))
    for n in range(len(back_s)):
        if 0 < n - LAG < len(later):
            gs = after(gs, later[n - LAG])
        gs = narrow_step(gs, back_s[n], sizes)
    gs, gu, gd = gs[0], gu[0], gd[0]

    def vector(v):
        return near_sum(gs[v, 128:144])

    return (
        out.reshape(tokens.shape),
        grad.reshape(tokens.shape),
        vector(0),
        vector(1),
        near_sum(jnp.transpose(gs[8 : 8 + experts, 128:144])),
        near_sum(gu[:, ff:]),
        vector(2),
        near_sum(gs[:, :128]),
        near_sum(gd[64:80]),
        vector(3),
        vector(4),
        vector(5),
        near_sum(gu[:, :ff]),
        near_sum(gs[0, 144:208]),
        near_sum(gd[:64]),
        vector(6),
    )


def solution(mesh):
    sizes = {name: mesh.shape[name] for name in ("seq", "batch")}
    both = ("seq", "batch")
    row = P("batch", "seq", None)
    vector, matrix = P(both), P(both, None)
    in_specs = (
        row,
        row,
        row,
        P("batch", None),
        vector,
        vector,
        matrix,
        matrix,
        vector,
        matrix,
        matrix,
        vector,
        vector,
        vector,
        matrix,
        vector,
        matrix,
        vector,
    )
    out_specs = (
        row,
        row,
        vector,
        vector,
        matrix,
        matrix,
        vector,
        matrix,
        matrix,
        vector,
        vector,
        vector,
        matrix,
        vector,
        matrix,
        vector,
    )
    return jax.shard_map(
        functools.partial(body, sizes),
        mesh=mesh,
        in_specs=in_specs,
        out_specs=out_specs,
        check_vma=False,
    )
```

```python
import functools

import jax
import jax.numpy as jnp
from jax import lax
from jax.experimental import pallas as pl
from jax.experimental.pallas import tpu as pltpu
from jax.sharding import PartitionSpec as P

EPS = 1e-05
NEG = -1e30
C0 = 0.7978845608028654
C1 = 0.7978845608028654 * 0.044715
PARTS = (4, 4)
LAG = 2
KVT = 3
GSW = 1
R = 2
FC = 32
FU = 4
RU = 2
CH = 32
UN = 16
SC = 64
SU = 4
SD = 64
SV = 8
VMEM_LIMIT = 52 * 1024 * 1024
SMALL_LIMIT = 24 * 1024 * 1024
F32 = jnp.float32
BF16 = jnp.bfloat16


def mm(a, b):
    return lax.dot_general(a, b, (((1,), (0,)), ((), ())), preferred_element_type=F32)


def mmt(a, b):
    return lax.dot_general(a, b, (((1,), (1,)), ((), ())), preferred_element_type=F32)


def fold8(v):
    return jnp.sum(v.reshape(v.shape[0] // 8, 8, v.shape[1]), axis=0)


def norm_parts(x):
    mean = jnp.mean(x, axis=-1, keepdims=True)
    xc = x - mean
    rstd = lax.rsqrt(jnp.mean(xc * xc, axis=-1, keepdims=True) + EPS)
    return xc * rstd, rstd


def norm_back(d, xhat, rstd):
    return rstd * (
        d
        - jnp.mean(d, axis=-1, keepdims=True)
        - xhat * jnp.mean(d * xhat, axis=-1, keepdims=True)
    )


def rel(bits, v):
    j = 0
    for src, dst in bits:
        j = j | (((v >> src) & 1) << dst)
    return j


def kernel_a(bits, nblk, parts, sc, own, got, tok, can, vec, bup, *kvs):
    *kvs, pack = kvs
    me = sc[0]
    pack[0 : nblk // 2] = own[...]
    pack[nblk // 2 :] = got[...]
    lane = lax.broadcasted_iota(jnp.int32, (16, 128), 1)
    for g in range(nblk // 8):
        rows = jnp.zeros((16, 128), F32)
        for i in range(8):
            b = g * 8 + i
            block = pack[rel(bits, me ^ b)]
            can[b * 16 : (b + 1) * 16, 0:640] = block[:, 0:640]
            tail = block[:, 640:768].astype(F32)
            rows = jnp.where(lane >> 4 == i, pltpu.roll(tail, i * 16, 1) if i else tail, rows)
            line = pltpu.roll(tail, 112 if i % 2 == 0 else 48, 1)
            wide = line if i % 2 == 0 else jnp.where(lane >= 64, line, wide)
            if i % 2:
                bup[:, (b // 2) * 128 : (b // 2 + 1) * 128] = wide[0:8]
        vec[:, g * 128 : (g + 1) * 128] = rows
    router = jnp.concatenate([vec[8:16, :], jnp.zeros((120, vec.shape[1]), F32)], axis=0)
    can[:, 640:768] = jnp.transpose(router).astype(BF16)
    gain = vec[0:1, :]
    shift = vec[1:2, :]
    row = 0
    for kv, count in zip(kvs, parts):
        for r in range(count):
            xhat, unused = norm_parts(tok[row].astype(F32))
            normed = (xhat * gain + shift).astype(BF16)
            kv[r] = mm(normed, can[:, 512:640]).astype(BF16)
            row += 1


def kernel_b(cfg, *refs):
    first, last, steps, bits_u, bits_d, gbits_u, gbits_d, nblk, nseq = cfg
    refs = list(refs)

    def take(n):
        got = refs[:n]
        del refs[:n]
        return got

    sc, tok, cot, idx, seg = take(5)
    kvs = take(nseq)
    can, vec, bup = take(3)
    u_own, u_got, d_own, d_got = take(4)
    acc_in = []
    if not first:
        acc_in = take(5)
        take(2)
    out_ref, part_ref = take(2)
    dkvs = take(nseq)
    (vacc,) = take(1)
    if last:
        gu_refs = take(2)
        gd_refs = take(2)
    acc_up, acc_dn, acc_wo, acc_wq = take(4)
    (
        wup,
        wdn,
        wo,
        xn,
        q_s,
        qp,
        dp,
        idx_b,
        gate_b,
        cd,
        inner,
        prob,
        score,
        wide1,
        wide2,
        mid,
        xh2,
        rs2,
        n2,
        mix,
        hid,
        gac,
        act,
        ghd,
        low1,
        gl,
        n2_t,
        cot_t,
        wsem,
        asem,
    ) = refs

    me = sc[0]
    place = sc[1]
    step = pl.program_id(0)
    tile = tok.shape[0]
    local = tile // R
    ch = CH
    nch = tile // ch
    lane128 = lax.broadcasted_iota(jnp.int32, (ch, 128), 1)
    upper = lane128 >= 64
    half = lane128 >> 6
    accs = (acc_up, acc_dn, acc_wo, acc_wq, vacc)

    @pl.when(step == 0)
    def _():
        for piece, base in ((u_own, 0), (u_got, u_own.shape[0])):
            for c in range(piece.shape[0]):
                blk = me ^ sum(((base + c) >> dst & 1) << src for src, dst in bits_u)
                pltpu.make_async_copy(
                    piece.at[c], wup.at[pl.ds(pl.multiple_of(blk * 16, 16), 16), :], wsem.at[0]
                ).start()
        for piece, base in ((d_own, 0), (d_got, d_own.shape[0])):
            for c in range(piece.shape[0]):
                blk = me ^ sum(((base + c) >> dst & 1) << src for src, dst in bits_d)
                pltpu.make_async_copy(
                    piece.at[c, pl.ds(0, 64), :],
                    wdn.at[pl.ds(pl.multiple_of(blk * 64, 64), 64), :],
                    wsem.at[1],
                ).start()
                pltpu.make_async_copy(
                    piece.at[c, pl.ds(64, 16), :],
                    wo.at[pl.ds(pl.multiple_of(blk * 16, 16), 16), :],
                    wsem.at[2],
                ).start()
        if first:
            for a in accs:
                a[...] = jnp.zeros_like(a)
        else:
            for n, a in enumerate(accs):
                pltpu.make_async_copy(acc_in[n], a, asem.at[n]).start()

    gain1 = vec[0:1, :]
    shift1 = vec[1:2, :]
    bias_q = vec[2:3, :]
    bias_o = vec[3:4, :]
    gain2 = vec[4:5, :]
    shift2 = vec[5:6, :]
    bias_d = vec[6:7, :]

    def norm_chunk(c, carry):
        sl = pl.ds(pl.multiple_of(c * ch, ch), ch)
        xhat, unused = norm_parts(tok[sl, :].astype(F32))
        xn[sl, :] = (xhat * gain1 + shift1).astype(BF16)
        return carry

    lax.fori_loop(0, nch, norm_chunk, 0, unroll=UN)
    q_s[...] = mm(xn[...], can[:, 0:512])
    low1[...] = mm(xn[...], can[:, 640:768])
    for r in range(R):
        for s in range(2):
            line = idx[r, s : s + 1, :].astype(F32)
            idx_b[s, r * local : (r + 1) * local, :] = jnp.transpose(
                jnp.broadcast_to(line, (128, local))
            ).astype(jnp.int32)

    def gate_chunk(c, carry):
        sl = pl.ds(pl.multiple_of(c * ch, ch), ch)
        logits = low1[sl, :]
        i0 = idx_b[0, sl, :]
        i1 = idx_b[1, sl, :]
        top = jnp.max(jnp.where(lane128 < 8, logits, -jnp.inf), axis=-1, keepdims=True)
        e0 = jnp.exp(jnp.sum(jnp.where(lane128 == i0, logits, 0.0), axis=-1, keepdims=True) - top)
        e1 = jnp.exp(jnp.sum(jnp.where(lane128 == i1, logits, 0.0), axis=-1, keepdims=True) - top)
        total = e0 + e1
        gate_b[0, sl, :] = jnp.broadcast_to(e0 / total, (ch, 128))
        gate_b[1, sl, :] = jnp.broadcast_to(e1 / total, (ch, 128))
        r = c // (local // ch)
        at = pl.multiple_of((c % (local // ch)) * ch, ch)
        f0 = jnp.zeros((ch, 128), F32)
        f1 = jnp.zeros((ch, 128), F32)
        for b in range(4):
            q = (q_s[sl, b * 128 : (b + 1) * 128] + bias_q[:, b * 128 : (b + 1) * 128]) * 0.125
            f0 = f0 + jnp.where(half + 2 * b == i0, q, 0.0)
            f1 = f1 + jnp.where(half + 2 * b == i1, q, 0.0)
        f0 = f0 + pltpu.roll(f0, 64, 1)
        f1 = f1 + pltpu.roll(f1, 64, 1)
        qp[r, pl.ds(at, ch), :] = jnp.where(upper, 0.0, f0).astype(BF16)
        qp[r, pl.ds(local + at, ch), :] = jnp.where(upper, 0.0, f1).astype(BF16)
        return carry

    lax.fori_loop(0, nch, gate_chunk, 0, unroll=UN)

    def attend(r, outer):
        for m in range(nseq):
            score[r, :, m * local : (m + 1) * local] = mmt(qp[r], kvs[m][r])
        seg_k = jnp.concatenate(
            [
                seg[r, :, pl.ds(pl.multiple_of((place ^ m) * local, 128), local)]
                for m in range(nseq)
            ],
            axis=1,
        )
        own = seg[r, :, pl.ds(pl.multiple_of(place * local, 128), local)].astype(F32)
        inner[pl.ds(pl.multiple_of(r * local, local), local), :] = jnp.transpose(
            jnp.broadcast_to(own, (128, local))
        )

        def soft_chunk(c, carry):
            at = pl.multiple_of(c * SC, SC)
            mine = pl.ds(pl.multiple_of(r * local + at, SC), SC)
            match = inner[mine, 0:1].astype(jnp.int32) == seg_k
            for s in range(2):
                sl = pl.ds(pl.multiple_of(s * local + at, SC), SC)
                sc_ = jnp.where(match, score[r, sl, :], NEG)
                num = jnp.exp(sc_ - jnp.max(sc_, axis=-1, keepdims=True))
                total = jnp.sum(num, axis=-1, keepdims=True)
                prob[r, sl, :] = (num * (1.0 / total)).astype(BF16)
            return carry

        lax.fori_loop(0, local // SC, soft_chunk, 0, unroll=SU)
        ctx = jnp.zeros((2 * local, 128), F32)
        for m in range(nseq):
            ctx = ctx + mm(prob[r, :, m * local : (m + 1) * local], kvs[m][r])
        up2 = lax.broadcasted_iota(jnp.int32, ctx.shape, 1) >= 64
        ctx = jnp.where(up2, ctx, 0.0)
        ctx = ctx + pltpu.roll(ctx, 64, 1)
        own_rows = pl.ds(pl.multiple_of(r * local, local), local)
        cd[0, own_rows, :] = ctx[:local]
        cd[1, own_rows, :] = ctx[local:]
        return outer

    for r in range(R):
        attend(r, 0)

    @pl.when(step == 0)
    def _():
        for n, w in enumerate((wup, wdn, wo)):
            pltpu.make_async_copy(w, w, wsem.at[n]).wait()
        if not first:
            for n, a in enumerate(accs):
                pltpu.make_async_copy(acc_in[n], a, asem.at[n]).wait()

    def mix_chunk(c, carry):
        sl = pl.ds(pl.multiple_of(c * ch, ch), ch)
        i0 = idx_b[0, sl, :]
        i1 = idx_b[1, sl, :]
        m0 = gate_b[0, sl, :] * cd[0, sl, :]
        m1 = gate_b[1, sl, :] * cd[1, sl, :]
        for b in range(4):
            mix[sl, b * 128 : (b + 1) * 128] = jnp.where(
                half + 2 * b == i0, m0, jnp.where(half + 2 * b == i1, m1, 0.0)
            ).astype(BF16)
        return carry

    lax.fori_loop(0, nch, mix_chunk, 0, unroll=UN)
    wide1[...] = mm(mix[...], wo[...])

    def mid_chunk(c, carry):
        sl = pl.ds(pl.multiple_of(c * ch, ch), ch)
        middle = tok[sl, :].astype(F32) + (wide1[sl, :] + bias_o)
        mid[sl, :] = middle
        xhat, rstd = norm_parts(middle)
        xh2[sl, :] = xhat
        rs2[sl, :] = jnp.broadcast_to(rstd, (ch, 128))
        n2[sl, :] = (xhat * gain2 + shift2).astype(BF16)
        return carry

    lax.fori_loop(0, nch, mid_chunk, 0, unroll=UN)

    n2_t[...] = jnp.transpose(n2[...])
    cot_t[...] = jnp.transpose(cot[...])
    width = hid.shape[2]
    wide1[...] = jnp.zeros_like(wide1)
    wide2[...] = jnp.zeros_like(wide2)

    def hidden_block(j, carry):
        js = slice(j * width, (j + 1) * width)
        k = j % 2
        hid[k] = mm(n2[...], wup[:, js])
        gac[k] = mmt(cot[...], wdn[js, :])
        bias = bup[0:1, js]
        total = jnp.zeros((8, width), F32)
        for c in range(tile // FC):
            sl = slice(c * FC, (c + 1) * FC)
            h = hid[k, sl, :] + bias
            h2 = h * h
            t = jnp.tanh(h * (C0 + C1 * h2))
            hh = 0.5 * h
            act[k, sl, :] = (hh + hh * t).astype(BF16)
            slope = (0.5 + 0.5 * t) + hh * (1.0 - t * t) * (C0 + (3.0 * C1) * h2)
            g = (gac[k, sl, :] * slope).astype(BF16)
            ghd[k, sl, :] = g
            total = total + fold8(g.astype(F32))
        vacc[(7 + j) * 8 : (8 + j) * 8, :] += total
        wide1[...] += mm(act[k], wdn[js, :])
        wide2[...] += mmt(ghd[k], wup[:, js])
        acc_up[:, js] += mm(n2_t[...], ghd[k])
        acc_dn[:, js] += mm(cot_t[...], act[k])
        return carry

    for j in range(wup.shape[1] // width):
        hidden_block(j, 0)

    def out_chunk(c, carry):
        sl = pl.ds(pl.multiple_of(c * ch, ch), ch)
        out_ref[sl, :] = (mid[sl, :] + (wide1[sl, :] + bias_d)).astype(BF16)
        ct = cot[sl, :].astype(F32)
        g = wide2[sl, :]
        xhat = xh2[sl, :]
        gm = ct + norm_back(g * gain2, xhat, rs2[sl, 0:1])
        mid[sl, :] = gm
        low = gm.astype(BF16)
        n2[sl, :] = low
        vacc[24:32, :] += fold8(low.astype(F32))
        vacc[32:40, :] += fold8(g * xhat)
        vacc[40:48, :] += fold8(g)
        vacc[48:56, :] += fold8(ct)
        return carry

    lax.fori_loop(0, nch, out_chunk, 0, unroll=UN)

    acc_wo[...] += mm(jnp.transpose(mix[...]), n2[...])
    wide1[...] = mmt(n2[...], wo[...])

    def gate_back_chunk(c, carry):
        sl = pl.ds(pl.multiple_of(c * ch, ch), ch)
        i0 = idx_b[0, sl, :]
        i1 = idx_b[1, sl, :]
        f0 = jnp.zeros((ch, 128), F32)
        f1 = jnp.zeros((ch, 128), F32)
        for b in range(4):
            g = wide1[sl, b * 128 : (b + 1) * 128]
            f0 = f0 + jnp.where(half + 2 * b == i0, g, 0.0)
            f1 = f1 + jnp.where(half + 2 * b == i1, g, 0.0)
        f0 = jnp.where(upper, f0 + pltpu.roll(f0, 64, 1), 0.0)
        f1 = jnp.where(upper, f1 + pltpu.roll(f1, 64, 1), 0.0)
        c0 = cd[0, sl, :]
        c1 = cd[1, sl, :]
        g0 = gate_b[0, sl, :]
        g1 = gate_b[1, sl, :]
        gg0 = jnp.sum(f0 * c0, axis=-1, keepdims=True)
        gg1 = jnp.sum(f1 * c1, axis=-1, keepdims=True)
        both = g0 * gg0 + g1 * gg1
        gl[sl, :] = jnp.where(
            lane128 == i0, g0 * (gg0 - both), jnp.where(lane128 == i1, g1 * (gg1 - both), 0.0)
        ).astype(BF16)
        d0 = (g0 * f0).astype(BF16)
        d1 = (g1 * f1).astype(BF16)
        r = c // (local // ch)
        at = pl.multiple_of((c % (local // ch)) * ch, ch)
        s0 = pl.ds(r * 2 * local + at, ch)
        s1 = pl.ds(r * 2 * local + local + at, ch)
        dp[r, pl.ds(at, ch), :] = d0
        dp[r, pl.ds(local + at, ch), :] = d1
        inner[s0, :] = jnp.broadcast_to(
            jnp.sum(d0.astype(F32) * c0, axis=-1, keepdims=True), (ch, 128)
        )
        inner[s1, :] = jnp.broadcast_to(
            jnp.sum(d1.astype(F32) * c1, axis=-1, keepdims=True), (ch, 128)
        )
        return carry

    lax.fori_loop(0, nch, gate_back_chunk, 0, unroll=UN)

    width = hid.shape[2]

    def attend_back(r, outer):
        for m in range(nseq):
            score[r, :, m * local : (m + 1) * local] = mmt(dp[r], kvs[m][r])
        dsc = (act, ghd)[r % 2]

        def score_chunk(c, carry):
            at = pl.multiple_of(c * SD, SD)
            sl = pl.ds(at, SD)
            inn = inner[pl.ds(pl.multiple_of(r * 2 * local + at, SD), SD), 0:1]
            for k in range(2):
                ks = slice(k * width, (k + 1) * width)
                dsc[k, sl, :] = (prob[r, sl, ks].astype(F32) * (score[r, sl, ks] - inn)).astype(BF16)
            return carry

        lax.fori_loop(0, 2 * local // SD, score_chunk, 0, unroll=SV)
        q_t = jnp.transpose(qp[r])
        d_t = jnp.transpose(dp[r])
        dq = jnp.zeros((2 * local, 128), F32)
        for m in range(nseq):
            k = m * local // width
            ks = slice(m * local - k * width, m * local - k * width + local)
            ds_m = dsc[k, :, ks]
            dq = dq + mm(ds_m, kvs[m][r])
            dkv_t = mm(q_t, ds_m) + mm(d_t, prob[r, :, m * local : (m + 1) * local])
            dkvs[m][r] = jnp.transpose(dkv_t).astype(BF16)
        up2 = lax.broadcasted_iota(jnp.int32, dq.shape, 1) >= 64
        dq = jnp.where(up2, 0.0, dq) * 0.125
        dq = dq + pltpu.roll(dq, 64, 1)
        own_rows = pl.ds(pl.multiple_of(r * local, local), local)
        cd[0, own_rows, :] = dq[:local]
        cd[1, own_rows, :] = dq[local:]
        return outer

    for r in range(R):
        attend_back(r, 0)

    def query_chunk(c, carry):
        sl = pl.ds(pl.multiple_of(c * ch, ch), ch)
        i0 = idx_b[0, sl, :]
        i1 = idx_b[1, sl, :]
        m0 = cd[0, sl, :]
        m1 = cd[1, sl, :]
        for b in range(4):
            low = jnp.where(
                half + 2 * b == i0, m0, jnp.where(half + 2 * b == i1, m1, 0.0)
            ).astype(BF16)
            mix[sl, b * 128 : (b + 1) * 128] = low
            vacc[16:24, b * 128 : (b + 1) * 128] += fold8(low.astype(F32))
        return carry

    lax.fori_loop(0, nch, query_chunk, 0, unroll=UN)
    xn_t = jnp.transpose(xn[...])
    acc_wq[...] += mm(xn_t, mix[...])
    vacc[88:104, :] += mm(jnp.transpose(gl[...])[0:16], xn[...])
    wide1[...] = mmt(mix[...], can[:, 0:512]) + mmt(gl[...], can[:, 640:768])

    def part_chunk(c, carry):
        sl = pl.ds(pl.multiple_of(c * ch, ch), ch)
        xhat, rstd = norm_parts(tok[sl, :].astype(F32))
        g = wide1[sl, :]
        part_ref[sl, :] = mid[sl, :] + norm_back(g * gain1, xhat, rstd)
        vacc[0:8, :] += fold8(g * xhat)
        vacc[8:16, :] += fold8(g)
        return carry

    lax.fori_loop(0, nch, part_chunk, 0, unroll=UN)

    if last:

        @pl.when(step == steps - 1)
        def _():
            for c in range(wdn.shape[0] // 128):
                cs = slice(c * 128, (c + 1) * 128)
                wdn[cs, :] = jnp.transpose(acc_dn[:, cs].astype(BF16))
            for j in range(nblk):
                h, i = j // (nblk // 2), j % (nblk // 2)
                b = me ^ sum((j >> dst & 1) << src for src, dst in gbits_u)
                rows = pl.ds(pl.multiple_of(b * 16, 16), 16)
                gu_refs[h][i, :, 0:2048] = acc_up[rows, :].astype(BF16)
                gu_refs[h][i, :, 2048:2560] = acc_wq[rows, :].astype(BF16)
                b = me ^ sum((j >> dst & 1) << src for src, dst in gbits_d)
                gd_refs[h][i, 0:64, :] = wdn[pl.ds(pl.multiple_of(b * 64, 64), 64), :]
                rows = pl.ds(pl.multiple_of(b * 16, 16), 16)
                gd_refs[h][i, 64:80, :] = acc_wo[rows, :].astype(BF16)


def kernel_e(cfg, *refs):
    first, last, steps, gbits, nblk, nseq = cfg
    refs = list(refs)

    def take(n):
        got = refs[:n]
        del refs[:n]
        return got

    sc, part, tok = take(3)
    dkvs = take(nseq)
    can, vec, vacc = take(3)
    acc_in = []
    if not first:
        acc_in = take(2)
        take(1)
    (out_ref,) = take(1)
    if last:
        gs_refs = take(2)
    acc_kv, acc_l = take(2)
    wide, xn, dk, small = refs
    me = sc[0]
    step = pl.program_id(0)
    tile = tok.shape[0]
    local = tile // R
    ch = CH
    nch = tile // ch
    gain = vec[0:1, :]
    shift = vec[1:2, :]

    @pl.when(step == 0)
    def _():
        if first:
            acc_kv[...] = jnp.zeros_like(acc_kv)
            acc_l[...] = jnp.zeros_like(acc_l)
        else:
            acc_kv[...] = acc_in[0][...]
            acc_l[...] = acc_in[1][...]

    for r in range(R):
        total = dkvs[0][r].astype(F32)
        for m in range(1, nseq):
            total = total + dkvs[m][r].astype(F32)
        dk[r * local : (r + 1) * local, :] = total.astype(BF16)
    wide[...] = mmt(dk[...], can[:, 512:640])

    def chunk(c, carry):
        sl = pl.ds(pl.multiple_of(c * ch, ch), ch)
        xhat, rstd = norm_parts(tok[sl, :].astype(F32))
        xn[sl, :] = (xhat * gain + shift).astype(BF16)
        g = wide[sl, :]
        out_ref[sl, :] = (part[sl, :] + norm_back(g * gain, xhat, rstd)).astype(BF16)
        acc_l[0:8, :] += fold8(g * xhat)
        acc_l[8:16, :] += fold8(g)
        return carry

    lax.fori_loop(0, nch, chunk, 0, unroll=UN)
    acc_kv[...] += mm(jnp.transpose(xn[...]), dk[...])

    if last:

        @pl.when(step == steps - 1)
        def _():
            row = lax.broadcasted_iota(jnp.int32, (16, 512), 0)
            table = jnp.zeros((16, 512), F32)
            for v in range(7):
                line = vacc[v * 8 : (v + 1) * 8, :]
                if v < 2:
                    line = line + acc_l[v * 8 : (v + 1) * 8, :]
                table = jnp.where(row == v, jnp.sum(line, axis=0, keepdims=True), table)
            router = vacc[88:104, :][0:8]
            table = table + jnp.concatenate([jnp.zeros((8, 512), F32), router], axis=0)
            ups = [
                jnp.sum(vacc[(7 + b) * 8 : (8 + b) * 8, :], axis=0, keepdims=True)
                for b in range(4)
            ]
            lane = lax.broadcasted_iota(jnp.int32, (16, 128), 1)
            first_row = lax.broadcasted_iota(jnp.int32, (16, 128), 0) == 0
            for b in range(nblk):
                g, i = b // 8, b % 8
                rows = table[:, g * 128 : (g + 1) * 128]
                if i:
                    rows = pltpu.roll(rows, 128 - i * 16, 1)
                c = b * 64 // 512
                at = (b * 64 % 512) // 128 * 128
                line = jnp.broadcast_to(ups[c][:, at : at + 128], (16, 128))
                line = pltpu.roll(line, 16 if b % 2 == 0 else 80, 1)
                tail = jnp.where(
                    lane < 16, rows, jnp.where(first_row & (lane < 80), line, 0.0)
                )
                small[b] = jnp.concatenate([acc_kv[b * 16 : (b + 1) * 16, :], tail], axis=1).astype(BF16)
            for j in range(nblk):
                h, i = j // (nblk // 2), j % (nblk // 2)
                b = me ^ sum((j >> dst & 1) << src for src, dst in gbits)
                gs_refs[h][i] = small[b]


def swap(x, hop, sizes):
    axis, mask = hop
    return lax.ppermute(x, axis, [(i, i ^ mask) for i in range(sizes[axis])])


def widen(x, order, sizes):
    for hop in order[:-1]:
        x = jnp.concatenate([x, swap(x, hop, sizes)], axis=0)
    return x, swap(x, order[-1], sizes)


def after(x, *deps):
    return lax.optimization_barrier((x,) + deps)[0]


def narrow_step(pair, hop, sizes):
    low, high = pair
    got = swap(high, hop, sizes)
    h = low.shape[0] // 2

    def add(sl):
        return low[sl].astype(F32) + got[sl].astype(F32)

    if h == 0:
        return add(slice(None))
    return add(slice(0, h)).astype(BF16), add(slice(h, 2 * h)).astype(BF16)


def whole(shape):
    zeros = (0,) * len(shape)
    return pl.BlockSpec(shape, lambda i: zeros, pipeline_mode=pl.Buffered(1))


def layer_calls(
    sc, tok, cot, idx, seg, kv_all, can, vec, bup, u_own, u_got, d_own, d_got,
    bits_u, bits_d, gbits_u, gbits_d, nblk, nseq, parts, moved=lambda dkv: None,
):
    d, ff, local = tok.shape[1], bup.shape[1], idx.shape[2]
    flat = tok.shape
    tile = R * local
    smem = pl.BlockSpec(memory_space=pltpu.SMEM)
    anywhere = pl.BlockSpec(memory_space=pl.ANY)
    params = pltpu.CompilerParams(vmem_limit_bytes=VMEM_LIMIT)
    shape = jax.ShapeDtypeStruct
    acc_shapes = (
        shape((d, ff), F32),
        shape((d, ff), F32),
        shape((d, d), F32),
        shape((d, d), F32),
    )
    vacc_shape = shape((104, d), F32)
    row0 = 0
    acc = None
    out = part = vacc = None
    for p, count in enumerate(parts):
        first, last = p == 0, p == len(parts) - 1
        steps = count // R
        base = row0 // R
        rowspec = pl.BlockSpec((tile, d), lambda i, base=base: (base + i, 0))
        kvspec = pl.BlockSpec((R, local, 128), lambda i: (i, 0, 0))
        ins = [sc, tok, cot, idx, seg] + kv_all[p] + [can, vec, bup, u_own, u_got, d_own, d_got]
        specs = [
            smem,
            rowspec,
            rowspec,
            pl.BlockSpec((R, 2, local), lambda i, base=base: (base + i, 0, 0)),
            pl.BlockSpec((R, 1, local * nseq), lambda i, base=base: (base + i, 0, 0)),
        ]
        specs += [kvspec] * nseq
        specs += [whole(can.shape), whole(vec.shape), whole(bup.shape)] + [anywhere] * 4
        alias = {}
        if not first:
            ins += list(acc) + [vacc, out, part]
            specs += [anywhere] * 7
            alias = {len(ins) - 2: 0, len(ins) - 1: 1}
        outs = [shape(flat, BF16), shape(flat, F32)]
        outs += [shape((count, local, 128), BF16)] * nseq + [vacc_shape]
        ospecs = [rowspec, rowspec] + [kvspec] * nseq + [whole(vacc_shape.shape)]
        scratch = []
        if last:
            sh_u, sh_d = (nblk // 2, 16, ff + d), (nblk // 2, 80, d)
            outs += [shape(sh_u, BF16)] * 2 + [shape(sh_d, BF16)] * 2
            ospecs += [whole(sh_u)] * 2 + [whole(sh_d)] * 2
            scratch += [pltpu.VMEM(a.shape, F32) for a in acc_shapes]
        else:
            outs += list(acc_shapes)
            ospecs += [whole(a.shape) for a in acc_shapes]
        wide = (tile, d)
        scratch += [
            pltpu.VMEM((d, ff), BF16),
            pltpu.VMEM((ff, d), BF16),
            pltpu.VMEM((d, d), BF16),
            pltpu.VMEM(wide, BF16),
            pltpu.VMEM(wide, F32),
            pltpu.VMEM((R, 2 * local, 128), BF16),
            pltpu.VMEM((R, 2 * local, 128), BF16),
            pltpu.VMEM((2, tile, 128), jnp.int32),
            pltpu.VMEM((2, tile, 128), F32),
            pltpu.VMEM((2, tile, 128), F32),
            pltpu.VMEM((2 * tile, 128), F32),
            pltpu.VMEM((R, 2 * local, nseq * local), BF16),
            pltpu.VMEM((R, 2 * local, nseq * local), F32),
            pltpu.VMEM(wide, F32),
            pltpu.VMEM(wide, F32),
            pltpu.VMEM(wide, F32),
            pltpu.VMEM(wide, F32),
            pltpu.VMEM((tile, 128), F32),
            pltpu.VMEM(wide, BF16),
            pltpu.VMEM(wide, BF16),
            pltpu.VMEM((2, tile, 512), F32),
            pltpu.VMEM((2, tile, 512), F32),
            pltpu.VMEM((2, tile, 512), BF16),
            pltpu.VMEM((2, tile, 512), BF16),
            pltpu.VMEM((tile, 128), F32),
            pltpu.VMEM((tile, 128), BF16),
            pltpu.VMEM((d, tile), BF16),
            pltpu.VMEM((d, tile), BF16),
            pltpu.SemaphoreType.DMA((3,)),
            pltpu.SemaphoreType.DMA((6,)),
        ]
        cfg = (
            first,
            last,
            steps,
            bits_u,
            bits_d,
            gbits_u,
            gbits_d,
            nblk,
            nseq,
        )
        got = pl.pallas_call(
            functools.partial(kernel_b, cfg),
            grid=(steps,),
            out_shape=tuple(outs),
            in_specs=specs,
            out_specs=tuple(ospecs),
            scratch_shapes=scratch,
            input_output_aliases=alias,
            compiler_params=params,
            name="layer",
        )(*ins)
        out, part = got[0], got[1]
        dkv = got[2 : 2 + nseq]
        moved(dkv)
        vacc = got[2 + nseq]
        acc = got[3 + nseq :]
        row0 += count

    return out, part, vacc, acc


def body(
    sizes,
    tokens,
    cotangent,
    expert_index,
    segments,
    ln1_gain,
    ln1_bias,
    w_router,
    w_query,
    b_query,
    w_keyval,
    w_out,
    b_out,
    ln2_gain,
    ln2_bias,
    w_up,
    b_up,
    w_down,
    b_down,
):
    nseq, nbatch = sizes["seq"], sizes["batch"]
    rows_dev, local, d = tokens.shape
    ff = w_up.shape[1]
    experts = w_router.shape[1]
    group = max(1, 16 // w_query.shape[0])
    high = nbatch // group
    nblk = nseq * high
    bidx = lax.axis_index("batch")
    sidx = lax.axis_index("seq")
    blk = sidx * high + bidx // group
    sc = jnp.stack([blk, sidx]).astype(jnp.int32)

    groups = [[g * group + i for i in range(group)] for g in range(high)]

    def near(w):
        if group == 1:
            return w
        return lax.all_gather(w, "batch", axis=0, tiled=True, axis_index_groups=groups)

    def near_sum(g):
        if group == 1:
            return g
        return lax.psum_scatter(
            g, "batch", scatter_dimension=0, tiled=True, axis_index_groups=groups
        )

    bb = [("batch", group << i) for i in range((high - 1).bit_length())]
    zz = [("seq", 1 << i) for i in range((nseq - 1).bit_length())]
    core, xy = bb[0], bb[1:]

    def bit_of(hop):
        axis, mask = hop
        step = mask // group if axis == "batch" else mask * high
        return step.bit_length() - 1

    def gather_bits(order):
        return tuple((bit_of(hop), i) for i, hop in enumerate(order))

    def scatter_bits(order):
        return tuple((bit_of(hop), len(order) - 1 - i) for i, hop in enumerate(order))

    def weave(a, b):
        out = []
        for i in range(max(len(a), len(b))):
            out += list(a[i : i + 1]) + list(b[i : i + 1])
        return out

    order_a = zz[::-1] + xy + [core]
    order_u = zz[::-1] + xy + [core]
    order_d = zz[::-1] + xy[::-1] + [core]
    back_u = [core] + xy[::-1] + zz
    back_d = [core] + xy + zz
    if GSW == 1:
        back_u = [core] + xy[::-1][:1] + zz[:1] + xy[::-1][1:] + zz[1:]
    if GSW == 2:
        back_u = [core] + xy[::-1][:1] + zz[:1] + zz[1:] + xy[::-1][1:]
    back_s = [core] + xy[::-1] + zz

    def grow(x, hop):
        return jnp.concatenate([x, swap(x, hop, sizes)], axis=0)

    table = jnp.concatenate(
        [
            near(v)[None]
            for v in (ln1_gain, ln1_bias, b_query, b_out, ln2_gain, ln2_bias, b_down, b_down)
        ]
        + [jnp.transpose(near(w_router))],
        axis=0,
    )
    tail = lax.pad(near(b_up)[None], jnp.zeros((), BF16), ((0, 15, 0), (0, 48, 0)))
    pack = jnp.concatenate([near(w_query), near(w_keyval), table, tail], axis=1)[None]
    u = near(w_up)[None]
    dn = jnp.concatenate([near(w_down), near(w_out)], axis=0)[None]
    nz = len(zz)
    for n in range(nz):
        pack = grow(pack, order_a[n])
        u = grow(u, order_u[n])
        dn = grow(dn, order_d[n])
    for hop in order_a[nz:-1]:
        pack = grow(pack, hop)
    u = grow(after(u, pack), order_u[nz])
    dn = grow(after(dn, pack), order_d[nz])
    packs = [pack, swap(pack, core, sizes)]

    smem = pl.BlockSpec(memory_space=pltpu.SMEM)
    anywhere = pl.BlockSpec(memory_space=pl.ANY)
    params = pltpu.CompilerParams(vmem_limit_bytes=SMALL_LIMIT)
    shape = jax.ShapeDtypeStruct

    can, vec, bup, *kv_parts = pl.pallas_call(
        functools.partial(kernel_a, gather_bits(order_a), nblk, PARTS),
        out_shape=(
            shape((d, 768), BF16),
            shape((16, d), F32),
            shape((8, ff), F32),
        )
        + tuple(shape((n, local, 128), BF16) for n in PARTS),
        in_specs=[smem] + [pl.BlockSpec(memory_space=pltpu.VMEM)] * 3,
        out_specs=tuple(pl.BlockSpec(memory_space=pltpu.VMEM) for unused in range(3 + len(PARTS))),
        scratch_shapes=[pltpu.VMEM((nblk, 16, 768), BF16)],
        compiler_params=params,
        name="project",
    )(sc, *packs, tokens)

    flat = (rows_dev * local, d)
    tok = tokens.reshape(flat)
    cot = cotangent.reshape(flat)
    idx = jnp.transpose(expert_index, (0, 2, 1))
    seg = segments[:, None, :]
    tile = R * local

    kv_all = []

    def gather_kv(kv):
        kv_all.append([kv] + [swap(kv, ("seq", m), sizes) for m in range(1, nseq)])

    gather_kv(kv_parts[0])
    u = after(u, kv_all[0][1])
    dn = after(dn, kv_all[0][1])
    for n in range(nz + 1, len(order_u) - 1):
        u = grow(u, order_u[n])
        dn = grow(dn, order_d[n])
    u = after(u, *kv_all[0])
    dn = after(dn, *kv_all[0])
    us = [u, swap(u, core, sizes)]
    ds = [dn, swap(dn, core, sizes)]
    for kv in kv_parts[1:]:
        gather_kv(after(kv, *kv_all[-1][:KVT]))
    dkv_all = []

    def moved(dkv):
        dkv_all.append([dkv[0]] + [swap(dkv[m], ("seq", m), sizes) for m in range(1, nseq)])

    out, part, vacc, acc = layer_calls(
        sc, tok, cot, idx, seg, kv_all, can, vec, bup, *us, *ds,
        gather_bits(order_u), gather_bits(order_d), scatter_bits(back_u), scatter_bits(back_d),
        nblk, nseq, PARTS, moved,
    )
    gu, gd = acc[0:2], acc[2:4]
    for n in range(len(PARTS) - 1):
        dkv_all[n] = [sum(v.astype(F32) for v in dkv_all[n]).astype(BF16)]
        gu, gd, dkv_all[n] = lax.optimization_barrier((gu, gd, dkv_all[n]))
    gu = narrow_step(gu, back_u[0], sizes)
    gd = narrow_step(gd, back_d[0], sizes)

    row0 = 0
    grad = None
    eacc = None
    for p, count in enumerate(PARTS):
        first, last = p == 0, p == len(PARTS) - 1
        steps = count // R
        base = row0 // R
        rowspec = pl.BlockSpec((tile, d), lambda i, base=base: (base + i, 0))
        kvspec = pl.BlockSpec((R, local, 128), lambda i: (i, 0, 0))
        if last:
            gu = narrow_step(gu, back_u[1], sizes)
            gd = narrow_step(gd, back_d[1], sizes)
        part = after(part, gu, gd)
        ins = [sc, part, tok] + list(dkv_all[p]) + [can, vec, vacc]
        specs = [smem, rowspec, rowspec] + [kvspec] * len(dkv_all[p])
        specs += [whole(can.shape), whole(vec.shape), whole(vacc.shape)]
        alias = {}
        if not first:
            ins += list(eacc) + [grad]
            specs += [whole((d, 128)), whole((16, d)), anywhere]
            alias = {len(ins) - 1: 0}
        outs = [shape(flat, BF16)]
        ospecs = [rowspec]
        scratch = []
        if last:
            outs += [shape((nblk // 2, 16, 256), BF16)] * 2
            ospecs += [whole((nblk // 2, 16, 256))] * 2
            scratch += [pltpu.VMEM((d, 128), F32), pltpu.VMEM((16, d), F32)]
        else:
            outs += [shape((d, 128), F32), shape((16, d), F32)]
            ospecs += [whole((d, 128)), whole((16, d))]
        scratch += [
            pltpu.VMEM((tile, d), F32),
            pltpu.VMEM((tile, d), BF16),
            pltpu.VMEM((tile, 128), BF16),
            pltpu.VMEM((nblk, 16, 256), BF16),
        ]
        cfg = (first, last, steps, scatter_bits(back_s), nblk, len(dkv_all[p]))
        got = pl.pallas_call(
            functools.partial(kernel_e, cfg),
            grid=(steps,),
            out_shape=tuple(outs),
            in_specs=specs,
            out_specs=tuple(ospecs),
            scratch_shapes=scratch,
            input_output_aliases=alias,
            compiler_params=params,
            name="finish",
        )(*ins)
        grad = got[0]
        eacc = got[1:]
        row0 += count
    gs = eacc
    gu, gd, unused = lax.optimization_barrier((gu, gd, dkv_all[-1]))
    later = [(gu, gd)]
    for n in range(2, len(back_u)):
        gu = narrow_step(gu, back_u[n], sizes)
        gd = narrow_step(gd, back_d[n], sizes)
        later.append((gu, gd))
    for n in range(len(back_s)):
        if 0 < n - LAG < len(later):
            gs = after(gs, later[n - LAG])
        gs = narrow_step(gs, back_s[n], sizes)
    gs, gu, gd = gs[0], gu[0], gd[0]

    def vector(v):
        return near_sum(gs[v, 128:144])

    return (
        out.reshape(tokens.shape),
        grad.reshape(tokens.shape),
        vector(0),
        vector(1),
        near_sum(jnp.transpose(gs[8 : 8 + experts, 128:144])),
        near_sum(gu[:, ff:]),
        vector(2),
        near_sum(gs[:, :128]),
        near_sum(gd[64:80]),
        vector(3),
        vector(4),
        vector(5),
        near_sum(gu[:, :ff]),
        near_sum(gs[0, 144:208]),
        near_sum(gd[:64]),
        vector(6),
    )


def solution(mesh):
    sizes = {name: mesh.shape[name] for name in ("seq", "batch")}
    both = ("seq", "batch")
    row = P("batch", "seq", None)
    vector, matrix = P(both), P(both, None)
    in_specs = (
        row,
        row,
        row,
        P("batch", None),
        vector,
        vector,
        matrix,
        matrix,
        vector,
        matrix,
        matrix,
        vector,
        vector,
        vector,
        matrix,
        vector,
        matrix,
        vector,
    )
    out_specs = (
        row,
        row,
        vector,
        vector,
        matrix,
        matrix,
        vector,
        matrix,
        matrix,
        vector,
        vector,
        vector,
        matrix,
        vector,
        matrix,
        vector,
    )
    return jax.shard_map(
        functools.partial(body, sizes),
        mesh=mesh,
        in_specs=in_specs,
        out_specs=out_specs,
        check_vma=False,
    )
```
